128 devices in a mesh: dp: 8 (over z, core), ctx: 16 (over x, y).
Axes of the slice: x: 4, y: 4, z: 4, core: 2. Of those that a mesh axis runs over, the one named last changes fastest.
Arguments:
- ssm_input: bfloat16 [32768, 8192], P(('dp', 'ctx')), may hold values from -6 to 6
- gate_input: bfloat16 [32768, 8192], P(('dp', 'ctx')), may hold values from -6 to 6
- write_basis: bfloat16 [32768, 1024], P(('dp', 'ctx')), may hold values from -2.5 to 2.5
- read_basis: bfloat16 [32768, 1024], P(('dp', 'ctx')), may hold values from -2.5 to 2.5
- step_size: bfloat16 [32768, 128], P(('dp', 'ctx')), may hold values from 0.01 to 0.5, as said below
- decay_rate: float32 [128], replicated, may hold values from 0.001 to 0.35, as said below
- skip_weight: float32 [128], replicated, may hold values from 0.5 to 1.5
- norm_gain: float32 [8192], replicated, may hold values from 0.1 to 1.9
- row_owner: int32 [32768, 1], P(('dp', 'ctx')), may hold values from 0 to 7; in each aligned block of 256 rows (0 to 255, 256 to 511, ...) at most 64 rows name the same one
- document_lengths: int32 [8, 8], P('dp'), may hold values from 1 to 4096, 8192 in all within a row
Outputs:
- layer_output: bfloat16 [32768, 8192], P(('dp', 'ctx'))
The draws below stay inside these ranges and needn't reach their ends.
Inputs may be any that keep to these rules, and one draw needn't show every extreme that they name: `row_owner`: within each device's block of 256 consecutive rows, no owner is named by more than 64 rows, a bound that some block reaches. `document_lengths`: each row sums to 8192; the largest entry of each row is 4096. `step_size`: Positive. `decay_rate`: Positive.
All inputs are finite; a program needn't handle non-finite values.
Results may differ from the reference program's by a relative error of at most 0.006.
Values may be sent and summed in bfloat16 or wider, within the bound.
A program may use at most 384 MiB of HBM per device.

```python
import math
import jax
import jax.numpy as jnp
import numpy as np
from jax import lax

HEADS = 128
HEAD_DIM = 64
STATE = 128
GROUPS = 8
TOK_DEV = 256
BLOCK = 512
DOCS = 8
ROWS = 32768
CAP = 64
SEQ = 8192
N_DP = 8
N_CTX = 16


def draw_step_size(key, part):
    key = jax.random.fold_in(key, 11)
    first_key, second_key = jax.random.split(key)
    rough = jax.random.uniform(first_key, (ROWS // TOK_DEV, TOK_DEV, HEADS), jnp.float32, 0.5, 1.5)
    device_scale = jnp.exp(jax.random.uniform(second_key, (ROWS // TOK_DEV, 1, 1), jnp.float32, jnp.log(0.5), jnp.log(2.0)))
    scaled = 0.1 * rough * device_scale
    return scaled.reshape(ROWS, HEADS).astype(jnp.bfloat16)


def draw_decay_rate(key, part):
    key = jax.random.fold_in(key, 23)
    first_key, second_key, third_key = jax.random.split(key, 3)
    slow_heads = jax.random.bernoulli(first_key, 0.5, (HEADS,))
    slow_rate = jnp.exp(jax.random.uniform(second_key, (HEADS,), jnp.float32, jnp.log(0.001), jnp.log(0.004)))
    spread_rate = jnp.exp(jax.random.uniform(third_key, (HEADS,), jnp.float32, jnp.log(0.004), jnp.log(0.35)))
    return jnp.where(slow_heads, slow_rate, spread_rate).astype(jnp.float32)


def steps_of(key, shape, shards, least, largest):
    loudness = 1.0
    for dim, blocks in shards:
        heights = jax.random.uniform(jax.random.fold_in(jax.random.fold_in(key, 6), dim), (blocks,), jnp.float32, least / len(shards), largest / len(shards))
        loudness = loudness * jnp.repeat(jnp.exp(heights), shape[dim] // blocks).reshape((-1,) + (1,) * (len(shape) - 1 - dim))
    return loudness


def length_profile(number_of, total, most, skew):
    loads = [(1 << 20) // math.isqrt(standing ** skew) + 1 for standing in range(2, number_of + 1)]
    surplus, given = total - most - (number_of - 1), [1] * (number_of - 1)
    while surplus > 0:
        candidates = [i for i in range(number_of - 1) if given[i] < most]
        pool, left = sum([loads[i] for i in candidates]), surplus
        for i in candidates:
            addition = min(most - given[i], max(1, left * loads[i] // pool), surplus)
            given[i] = given[i] + addition
            surplus = surplus - addition
    return np.array([most] + given)


def ragged(stream_key, amount, total, bound, slope):
    if amount == 2:
        one = jax.random.randint(stream_key, (), max(1, total - bound), min(bound, total - 1) + 1)
        return jnp.stack([one, total - one])
    tallies = jnp.asarray(length_profile(amount, total, bound, slope), jnp.int32)
    couples = (amount - 1) // 2
    source_of, sink = tallies[1:1 + 2 * couples:2], tallies[2:2 + 2 * couples:2]
    room = jnp.minimum(source_of - 1, bound - sink)
    passed = jax.random.randint(jax.random.fold_in(stream_key, 1), (couples,), 0, 1 << 20) % (room + 1)
    tallies = tallies.at[1:1 + 2 * couples:2].set(source_of - passed).at[2:2 + 2 * couples:2].set(sink + passed)
    return tallies[jax.random.permutation(jax.random.fold_in(stream_key, 2), amount)]


def deal_out(own_key, own, number, rows, count, top, bound, slope):
    order = jax.random.permutation(own_key, count)
    crowded, ordinary = shares(count, rows * top, bound, slope, True), shares(count, rows * top, bound, slope, False)
    places = jnp.arange(count)

    def named(sizes, rotation):
        used = int((sizes > 0).sum())
        fixed = max(1, used // 4)
        shifted = fixed + (places - fixed + rotation * (used - fixed)) % max(1, count - fixed)
        return jnp.zeros((count,), jnp.int32).at[order[jnp.where(places < fixed, places, shifted)]].set(jnp.asarray(sizes, jnp.int32))

    sizes = jnp.where(number % 4 == 0, named(crowded, number // 4), named(ordinary, number - number // 4 - 1))
    mixed = jax.random.permutation(jax.random.fold_in(own, 3), count)
    source_of, taker = mixed[0:count // 2 * 2:2], mixed[1:count // 2 * 2:2]
    room = jnp.minimum(sizes[source_of] - 1, bound - sizes[taker]) // 2
    room = jnp.where((source_of == order[0]) | (taker == order[0]) | (sizes[taker] == 0), 0, jnp.maximum(room, 0))
    shifted = jax.random.randint(jax.random.fold_in(own, 4), (count // 2,), 0, 1 << 20) % (room + 1)
    sizes = sizes.at[source_of].add(-shifted).at[taker].add(shifted)
    labels = jnp.searchsorted(jnp.cumsum(sizes), jnp.arange(rows * top), side="right").astype(jnp.int32)
    grid = labels.reshape(top, rows).T
    grid = grid[jax.random.permutation(jax.random.fold_in(own, 1), rows)]
    rotation = jax.random.randint(jax.random.fold_in(own, 2), (rows, 1), 0, top)
    return jnp.take_along_axis(grid, (jnp.arange(top)[None, :] + rotation) % top, axis=1)


def shares(number_of, total, reach, skew, full):
    weights = [(1 << 20) // math.isqrt(rank ** skew) + 1 for rank in range(1, number_of + 1)]
    largest = reach if full else min(reach, max(-(-total // number_of), total * weights[0] // sum(weights)))
    least = 1 if total - largest >= number_of - 1 else 0
    counts, surplus = [largest] + [least] * (number_of - 1), total - largest - least * (number_of - 1)
    while surplus > 0:
        movable = [i for i in range(1, number_of) if counts[i] < largest] or [i for i in range(1, number_of) if counts[i] < reach]
        mass, remaining = sum([weights[i] for i in movable]), surplus
        for i in movable:
            extra = min(reach - counts[i], max(1, remaining * weights[i] // mass), surplus)
            counts[i] = counts[i] + extra
            surplus = surplus - extra
    return np.array(counts)


def scatter_about(key, dims, scale, reach, cuts=(), kind=jnp.bfloat16):
    values = jax.random.normal(key, dims, jnp.float32) * scale
    if len(cuts) > 0:
        values = steps_of(key, dims, cuts, -0.22, 0.18) * values
    return jnp.clip(values, min=-reach, max=reach).astype(kind)


def setup_inputs(seed: int = 0) -> dict:
    seeds = jax.random.split(jax.random.key(seed), 11)
    ssm_input = scatter_about(seeds[0], (ROWS, HEADS * HEAD_DIM), 1.0, 6.0, ((0, 128),))
    gate_input = scatter_about(seeds[1], (ROWS, HEADS * HEAD_DIM), 1.0, 6.0, ((0, 128),))
    write_basis = scatter_about(seeds[2], (ROWS, GROUPS * STATE), 0.35, 2.5, ((0, 128),))
    read_basis = scatter_about(seeds[3], (ROWS, GROUPS * STATE), 0.35, 2.5, ((0, 128),))
    step_size = draw_step_size(jax.random.fold_in(seeds[10], 71), 0)
    decay_rate = draw_decay_rate(jax.random.fold_in(seeds[10], 71), 0)
    skip_weight = jnp.clip(jax.random.uniform(seeds[6], (HEADS,), jnp.float32, 0.5, 1.5), 0.5, 1.5)
    norm_gain = jnp.clip(1.0 + 0.18 * jax.random.normal(seeds[7], (HEADS * HEAD_DIM,), jnp.float32), 0.1, 1.9)
    row_owner_keys = jax.random.split(jax.random.fold_in(seeds[8], 1), ROWS // TOK_DEV)
    row_owner_turns = jax.random.permutation(jax.random.fold_in(seeds[8], 3), ROWS // TOK_DEV)
    row_owner = jax.vmap(lambda own, number: deal_out(jax.random.fold_in(seeds[8], 2), own, number, TOK_DEV, N_DP, 1, CAP, 2))(row_owner_keys, row_owner_turns).reshape((ROWS, 1))
    document_lengths = jax.vmap(lambda own: ragged(own, DOCS, SEQ, N_CTX * TOK_DEV, 2))(jax.random.split(seeds[9], N_DP)).reshape((N_DP, DOCS)).astype(jnp.int32)
    return {"ssm_input": ssm_input, "gate_input": gate_input, "write_basis": write_basis, "read_basis": read_basis, "step_size": step_size, "decay_rate": decay_rate, "skip_weight": skip_weight, "norm_gain": norm_gain, "row_owner": row_owner, "document_lengths": document_lengths}


EPSILON = 1e-05

def rounded(values):
    return lax.optimization_barrier(values.astype(jnp.bfloat16)).astype(jnp.float32)

def segment_of(positions, lengths):
    starts = jnp.cumsum(lengths) - lengths
    return lax.optimization_barrier(jnp.sum((positions[:, None] >= starts[None, :]).astype(jnp.int32), axis=1)) - 1

def slot_positions(row_owner):
    destination = row_owner[:, 0].reshape(N_DP, N_CTX, TOK_DEV)
    owner_table = (destination[..., None] == jnp.arange(N_DP, dtype=jnp.int32)).astype(jnp.int32)
    owner_rank = lax.optimization_barrier(jnp.sum((jnp.cumsum(owner_table, axis=2) - 1) * owner_table, axis=3))
    source_rank = jnp.arange(N_DP, dtype=jnp.int32)[:, None, None]
    column = jnp.arange(N_CTX, dtype=jnp.int32)[None, :, None]
    position = column * (N_DP * CAP) + source_rank * CAP + owner_rank
    return (destination.reshape(-1).astype(jnp.int32), position.reshape(-1).astype(jnp.int32))

def block_terms(values, write_rows, read_rows, step_rows, decay_rate, skip_weight, segments, before, carried):
    block_size, head_count = step_rows.shape
    per_group = head_count // GROUPS
    head_width = values.shape[1] // head_count
    step_values = step_rows.astype(jnp.float32)
    cumulative = jnp.cumsum(-decay_rate[None, :] * step_values, axis=0)
    slot_order = jnp.arange(block_size)
    allowed = (slot_order[:, None] >= slot_order[None, :]) & (segments[:, None] == segments[None, :])
    grouped_values = values.reshape(block_size, GROUPS, per_group, head_width).astype(jnp.float32)
    writes_grouped = write_rows.reshape(block_size, GROUPS, -1)
    reads_grouped = read_rows.reshape(block_size, GROUPS, -1)
    inner_parts = []
    for group_index in range(GROUPS):
        head_start = group_index * per_group
        intersection = jnp.dot(reads_grouped[:, group_index], writes_grouped[:, group_index].T, preferred_element_type=jnp.float32)
        local_cum = cumulative[:, head_start:head_start + per_group].T
        exponent = jnp.where(allowed[None], local_cum[:, :, None] - local_cum[:, None, :], -jnp.inf)
        local_steps = step_values[:, head_start:head_start + per_group].T
        scores = rounded(intersection[None] * jnp.exp(exponent) * local_steps[:, None, :])
        inner_parts.append(jnp.einsum('hqs,shp->qhp', scores, grouped_values[:, group_index], precision=lax.Precision.HIGHEST))
    inner_sum = jnp.stack(inner_parts, axis=1).reshape(block_size, head_count, head_width)
    keep_end = (segments == segments[-1]).astype(jnp.float32)
    weights = jnp.exp(cumulative[-1][None, :] - cumulative) * step_values * keep_end[:, None]
    weighted = rounded(weights.reshape(block_size, GROUPS, per_group, 1) * write_rows.reshape(block_size, GROUPS, 1, -1).astype(jnp.float32))
    state_sum = jnp.einsum('sghp,sghn->ghpn', grouped_values, weighted, precision=lax.Precision.HIGHEST).reshape(head_count, head_width, -1)
    block_decay = jnp.exp(cumulative[-1]) * (segments[-1] == before).astype(jnp.float32)
    factor = jnp.exp(cumulative) * (segments == before).astype(jnp.float32)[:, None]
    rounded_state = rounded(carried).reshape(GROUPS, per_group, head_width, -1)
    carried_part = jnp.einsum('qgn,ghpn->qghp', reads_grouped.astype(jnp.float32), rounded_state, precision=lax.Precision.HIGHEST).reshape(block_size, head_count, head_width)
    direct = skip_weight[None, :, None] * values.reshape(block_size, head_count, head_width).astype(jnp.float32)
    mixed_rows = (inner_sum + carried_part * factor[:, :, None] + direct).reshape(block_size, -1).astype(jnp.bfloat16)
    next_state = block_decay[:, None, None] * carried + state_sum
    return (mixed_rows, next_state)

def mix_sequence(values, write_rows, read_rows, step_rows, lengths, decay_rate, skip_weight):
    slot_total = values.shape[0]
    block_count = slot_total // BLOCK
    segments_all = segment_of(jnp.arange(-1, slot_total, dtype=jnp.int32), lengths)
    segments = segments_all[1:].reshape(block_count, BLOCK)
    befores = segments_all[:-1].reshape(block_count, BLOCK)[:, 0]
    head_count = step_rows.shape[1]

    def advance(carried, pieces):
        mixed_rows, next_state = block_terms(pieces[0], pieces[1], pieces[2], pieces[3], decay_rate, skip_weight, pieces[4], pieces[5], carried)
        return (next_state, mixed_rows)
    start_state = jnp.zeros((head_count, values.shape[1] // head_count, write_rows.shape[1] // GROUPS), jnp.float32)
    pieces = (values.reshape(block_count, BLOCK, -1), write_rows.reshape(block_count, BLOCK, -1), read_rows.reshape(block_count, BLOCK, -1), step_rows.reshape(block_count, BLOCK, -1), segments, befores)
    final_state, mixed_blocks = lax.scan(advance, start_state, pieces)
    return mixed_blocks.reshape(slot_total, -1)

def reference(ssm_input, gate_input, write_basis, read_basis, step_size, decay_rate, skip_weight, norm_gain, row_owner, document_lengths):
    row_total = ssm_input.shape[0]
    destination, position = slot_positions(row_owner)
    slot_table = jnp.full((N_DP, SEQ), row_total, jnp.int32).at[destination, position].set(jnp.arange(row_total, dtype=jnp.int32))

    def padded(values):
        return jnp.concatenate([values, jnp.zeros((1, values.shape[1]), values.dtype)], axis=0)
    input_pad = padded(ssm_input)
    write_pad = padded(write_basis)
    read_pad = padded(read_basis)
    step_pad = padded(step_size)

    def one_sequence(pieces):
        slot_rows, lengths = pieces
        return mix_sequence(input_pad[slot_rows], write_pad[slot_rows], read_pad[slot_rows], step_pad[slot_rows], lengths, decay_rate, skip_weight)
    mixed_all = lax.map(one_sequence, (slot_table, document_lengths))
    ssd_rows = mixed_all[destination, position]
    gated_rows = ssd_rows.astype(jnp.float32) * jax.nn.silu(gate_input.astype(jnp.float32))
    grouped = gated_rows.reshape(row_total, GROUPS, -1)
    inverse_rms = lax.rsqrt(lax.optimization_barrier(jnp.mean(grouped * grouped, axis=2, keepdims=True)) + EPSILON)
    return ((grouped * inverse_rms).reshape(row_total, -1) * norm_gain[None, :]).astype(jnp.bfloat16)
```

```python
import jax
import jax.numpy as jnp
from jax import lax
from jax.experimental import pallas as pl
from jax.experimental.pallas import tpu as pltpu
from jax.sharding import PartitionSpec as P

GROUPS = 8
BLOCK = 512
EPSILON = 1e-05
CHUNKS = 4
N_DP = 8
N_CTX = 16
ROWS = 256
HEADS = 16
WIDTH = 1024 // CHUNKS
STATE = 128
DOCS = 8
SLOTS = 64
MESH = pl.DeviceIdType.MESH
F32 = jnp.float32
BF16 = jnp.bfloat16


def dot(a, b, dims=((1,), (0,)), precision=None):
    return lax.dot_general(a, b, (dims, ((), ())), precision=precision, preferred_element_type=F32)


def exact(a, b, dims=((1,), (0,))):
    return dot(a, b, dims, lax.Precision.HIGHEST)


def thirds(value):
    high = value.astype(BF16).astype(F32)
    middle = (value - high).astype(BF16).astype(F32)
    low = (value - high - middle).astype(BF16).astype(F32)
    return high, middle, low


def iota(shape, dim):
    return lax.broadcasted_iota(jnp.int32, shape, dim)


def kernel(
    x_ref,
    gate_ref,
    write_ref,
    read_ref,
    packet_ref,
    rate_ref,
    skip_ref,
    gain_ref,
    out_ref,
    gate_buf,
    meta,
    writes,
    reads,
    xs,
    aux,
    aux_in,
    sums,
    sums_in,
    states,
    states_in,
    mixed,
    mixed_in,
    scores,
    scaled,
    writes_t,
    reads_m,
    factors,
    keys_row,
    keys_col,
    spread,
    local_sem,
    send_sem,
    recv_sem,
    x_send,
    x_recv,
    s_send,
    s_recv,
    h_send,
    h_recv,
    y_send,
    y_recv,
):
    me = lax.axis_index("dp")
    col = lax.axis_index("ctx")

    def remote(src, dst, send, recv, axis, peer):
        return pltpu.make_async_remote_copy(
            src_ref=src,
            dst_ref=dst,
            send_sem=send,
            recv_sem=recv,
            device_id={axis: peer},
            device_id_type=MESH,
        )

    def lanes(ref, start, width):
        return ref.at[:, pl.ds(pl.multiple_of(start, 128), width)]

    own = [
        pltpu.make_async_copy(packet_ref.at[me], meta.at[me], local_sem.at[0]),
        pltpu.make_async_copy(lanes(write_ref, me * STATE, STATE), writes.at[me], local_sem.at[1]),
        pltpu.make_async_copy(lanes(read_ref, me * STATE, STATE), reads.at[me], local_sem.at[2]),
        pltpu.make_async_copy(gate_ref, gate_buf, local_sem.at[3]),
    ]
    own_x = [
        pltpu.make_async_copy(
            lanes(x_ref, me * 1024 + c * WIDTH, WIDTH), xs.at[c, me], local_sem.at[4 + c]
        )
        for c in range(CHUNKS)
    ]
    for copy in own[:3] + own_x + own[3:]:
        copy.start()

    barrier = pltpu.get_barrier_semaphore()
    for d in range(1, N_DP):
        pl.semaphore_signal(
            barrier, inc=1, device_id={"dp": lax.rem(me + d, N_DP)}, device_id_type=MESH
        )
    for d in range(1, N_CTX):
        pl.semaphore_signal(
            barrier, inc=1, device_id={"ctx": lax.rem(col + d, N_CTX)}, device_id_type=MESH
        )
    pl.semaphore_wait(barrier, N_DP + N_CTX - 2)

    for d in range(1, N_DP):
        peer = lax.rem(me + d, N_DP)
        remote(
            packet_ref.at[peer], meta.at[me], send_sem.at[0], recv_sem.at[0], "dp", peer
        ).start()
    for d in range(1, N_DP):
        peer = lax.rem(me + d, N_DP)
        remote(
            lanes(write_ref, peer * STATE, STATE),
            writes.at[me],
            send_sem.at[1],
            recv_sem.at[1],
            "dp",
            peer,
        ).start()
        remote(
            lanes(read_ref, peer * STATE, STATE),
            reads.at[me],
            send_sem.at[2],
            recv_sem.at[2],
            "dp",
            peer,
        ).start()
    for c in range(CHUNKS):
        for d in range(1, N_DP):
            peer = lax.rem(me + d, N_DP)
            remote(
                lanes(x_ref, peer * 1024 + c * WIDTH, WIDTH),
                xs.at[c, me],
                x_send.at[c],
                x_recv.at[c],
                "dp",
                peer,
            ).start()

    row = iota((128, WIDTH), 0)
    for c in range(CHUNKS):
        head = c * (HEADS // CHUNKS) + iota((128, WIDTH), 1) // 64
        named = lax.rem(row, HEADS) == head
        spread[0, c] = jnp.where(named & (row < 48), 1.0, 0.0).astype(BF16)
        spread[1, c] = jnp.where(named & (row >= 48) & (row < 96), 1.0, 0.0).astype(BF16)

    def arrived(ref, count, sem):
        part = ref.at[pl.ds(0, count)]
        pltpu.make_async_copy(part, part, sem).wait()

    own[0].wait()
    arrived(meta, N_DP - 1, recv_sem.at[0])
    first_slot = (col * BLOCK).astype(F32)

    owners = meta[:, 16, :]
    lengths = meta[:, 17, :]
    starts = []
    total = jnp.zeros((N_DP, 1), F32)
    for d in range(DOCS):
        starts.append(total)
        total = total + lengths[:, d : d + 1]
    sequence = iota((N_DP, 1), 0).astype(F32)
    table = jnp.where(
        owners[:, None, :] == iota((N_DP, N_DP, ROWS), 1).astype(F32), 1.0, 0.0
    )
    earlier = jnp.where(iota((ROWS, ROWS), 0) < iota((ROWS, ROWS), 1), 1.0, 0.0)
    counts = dot(table.reshape(N_DP * N_DP, ROWS).astype(BF16), earlier.astype(BF16))
    rank = jnp.sum(table * counts.reshape(N_DP, N_DP, ROWS), axis=1)
    slot = first_slot + (iota((N_DP, ROWS), 0) * SLOTS).astype(F32) + rank
    segment = jnp.zeros((N_DP, N_DP, ROWS), F32)
    before = jnp.zeros((N_DP, 1), F32)
    end = jnp.zeros((N_DP, 1), F32)
    for d in range(DOCS):
        segment = segment + jnp.where(slot[:, None, :] >= starts[d][None], 1.0, 0.0)
        before = before + jnp.where(first_slot - 1.0 >= starts[d], 1.0, 0.0)
        end = end + jnp.where(first_slot + (BLOCK - 1.0) >= starts[d], 1.0, 0.0)
    key = owners * 16.0 + jnp.sum(table * segment, axis=1)
    key_before = sequence * 16.0 + before
    key_end = sequence * 16.0 + end
    same_document = jnp.where(key_before == key_end, 1.0, 0.0)
    keys_row[...] = key
    key_t = key.T
    owner_t = owners.T

    rate_row = rate_ref[pl.ds(me, 1), :]
    rate = jnp.sum(
        jnp.where(iota((HEADS, HEADS), 0) == iota((HEADS, HEADS), 1), rate_row, 0.0),
        axis=1,
        keepdims=True,
    )
    not_later = iota((ROWS, ROWS), 0) <= iota((ROWS, ROWS), 1)
    sofar = jnp.zeros((HEADS, N_DP), F32)
    whole_t = jnp.zeros((N_DP, HEADS), F32)
    running = []
    for i in range(N_DP):
        keys_col[i] = jnp.broadcast_to(key_t[:, i : i + 1], (ROWS, 128))
        step = meta[i, 0:HEADS, :].astype(BF16)
        owned = table[i]
        same = jnp.where((owner_t[:, i : i + 1] == owners[i : i + 1, :]) & not_later, 1.0, 0.0)
        running.append(dot(step, same.astype(BF16)) + exact(sofar, owned))
        sofar = sofar + dot(step, owned.astype(BF16), ((1,), (1,)))
        whole_t = whole_t + dot(owned.astype(BF16), step, ((1,), (1,)))
    middle = -0.5 * rate * sofar
    for i in range(N_DP):
        exponent = -rate * running[i] - exact(middle, table[i])
        rising = thirds(jnp.exp(-exponent) * meta[i, 0:HEADS, :])
        falling = thirds(jnp.exp(exponent))
        stack = jnp.concatenate(falling + rising + (jnp.zeros((32, ROWS), F32),), axis=0)
        factors[i] = stack.T.astype(BF16)
    middle_t = -0.5 * whole_t * rate_row
    half_decay = thirds(jnp.exp(middle_t))
    full_decay = thirds(jnp.exp(2.0 * middle_t) * same_document)
    for c in range(CHUNKS):
        heads = spread[0, c, 0:HEADS, :]
        half = sum(dot(part.astype(BF16), heads) for part in half_decay)
        full = sum(dot(part.astype(BF16), heads) for part in full_decay)
        for k in range(N_DP):
            aux[k, 0:1, c * WIDTH : (c + 1) * WIDTH] = full[k : k + 1, :]
            aux[k, 1:2, c * WIDTH : (c + 1) * WIDTH] = half[k : k + 1, :]
    for k in range(N_DP):
        aux[k, 2:8, :] = jnp.zeros((6, 1024), F32)
    for d in range(1, N_CTX):
        peer = lax.rem(col + d, N_CTX)
        remote(
            aux.at[peer // 2], aux_in.at[col], send_sem.at[3], recv_sem.at[3], "ctx", peer
        ).start()
    aux_in[col] = aux[col // 2]

    own[1].wait()
    arrived(writes, N_DP - 1, recv_sem.at[1])
    for i in range(N_DP):
        flipped = writes[i].astype(F32).T
        for k in range(N_DP):
            kept = keys_row[i : i + 1, :] == key_end[k : k + 1, :]
            writes_t[k, :, i * ROWS : (i + 1) * ROWS] = jnp.where(kept, flipped, 0.0).astype(BF16)
    own[2].wait()
    arrived(reads, N_DP - 1, recv_sem.at[2])

    for i in range(N_DP):
        block = reads[i].astype(F32)
        for k in range(N_DP):
            kept = keys_col[i] == key_before[k : k + 1, :]
            reads_m[i, :, k * STATE : (k + 1) * STATE] = jnp.where(kept, block, 0.0).astype(BF16)

    ordered = iota((ROWS, ROWS), 0) >= iota((ROWS, ROWS), 1)

    def score_rows(i, carry):
        key_q = keys_col[i][:, 0:1]
        block = reads[i]

        def score(j, carry):
            raw = dot(block, writes[j], ((1,), (1,)))
            kept = (key_q == keys_row[pl.ds(j, 1), :]) & (ordered | (j < i))
            scores[i, :, pl.ds(pl.multiple_of(j * ROWS, ROWS), ROWS)] = jnp.where(
                kept, raw, 0.0
            ).astype(BF16)
            return carry

        return lax.fori_loop(0, i + 1, score, carry)

    lax.fori_loop(0, N_DP, score_rows, 0)

    def summarize(c):
        pltpu.make_async_copy(xs.at[0, 0], xs.at[0, 0], local_sem.at[4 + c]).wait()
        arrived(xs.at[c], N_DP - 1, x_recv.at[c])

        def scale(i, carry):
            factor = dot(factors[i], spread[1, c])
            scaled[c, pl.ds(pl.multiple_of(i * ROWS, ROWS), ROWS), :] = (
                xs[c, i].astype(F32) * factor
            ).astype(BF16)
            return carry

        lax.fori_loop(0, N_DP, scale, 0)

        def collect(k, carry):
            part = dot(writes_t[k], scaled[c])
            half = aux[k, 1:2, pl.ds(pl.multiple_of(c * WIDTH, WIDTH), WIDTH)]
            part = (part * half).astype(BF16)
            sums[c, 2 * k] = part[0:64]
            sums[c, 2 * k + 1] = part[64:128]
            return carry

        lax.fori_loop(0, N_DP, collect, 0)
        for d in range(1, N_CTX):
            peer = lax.rem(col + d, N_CTX)
            remote(
                sums.at[c, peer], sums_in.at[c, col], s_send.at[c], s_recv.at[c], "ctx", peer
            ).start()
        sums_in[c, col] = sums[c, col]

    def carry_on(c):
        @pl.when(c == 0)
        def _():
            arrived(aux_in, N_CTX - 1, recv_sem.at[3])

        arrived(sums_in.at[c], N_CTX - 1, s_recv.at[c])
        window = pl.ds(pl.multiple_of(c * WIDTH, WIDTH), WIDTH)

        def advance(j, held):
            states[c, j] = (held * aux_in[j, 1:2, window]).astype(BF16)
            return held * aux_in[j, 0:1, window] + sums_in[c, j].astype(F32)

        lax.fori_loop(0, N_CTX, advance, jnp.zeros((64, WIDTH), F32))
        for d in range(1, N_CTX):
            peer = lax.rem(col + d, N_CTX)
            remote(
                states.at[c, peer], states_in.at[c, col], h_send.at[c], h_recv.at[c], "ctx", peer
            ).start()
        states_in[c, col] = states[c, col]

    def mix(c):
        arrived(states_in.at[c], N_CTX - 1, h_recv.at[c])
        carried = states_in[c].reshape(N_DP * STATE, WIDTH)
        skip = skip_ref[pl.ds(me, 1), pl.ds(pl.multiple_of(c * WIDTH, WIDTH), WIDTH)]
        for i in range(N_DP):
            reach = (i + 1) * ROWS
            both = dot(scores[i, :, 0:reach], scaled[c, 0:reach, :]) + dot(reads_m[i], carried)
            factor = dot(factors[i], spread[0, c])
            mixed[c, i] = (both * factor + skip * xs[c, i].astype(F32)).astype(BF16)

            @pl.when(me != i)
            def _():
                remote(
                    mixed.at[c, i], mixed_in.at[c, me], y_send.at[c], y_recv.at[c], "dp", i
                ).start()

        mixed_in[c, me] = mixed[c, me]

    def step(s, carry):
        @pl.when(s < CHUNKS)
        def _():
            summarize(s)

        @pl.when(s > 0)
        def _():
            mix(s - 1)

        @pl.when(s < CHUNKS)
        def _():
            carry_on(s)

        return carry

    lax.fori_loop(0, CHUNKS + 1, step, 0)

    own[3].wait()
    for c in range(CHUNKS):
        arrived(mixed_in.at[c], N_DP - 1, y_recv.at[c])

    def finish(g, carry):
        gated = []
        squares = jnp.zeros((ROWS, 1), F32)
        for c in range(CHUNKS):
            place = pl.ds(pl.multiple_of(g * 1024 + c * WIDTH, WIDTH), WIDTH)
            gate = gate_buf[:, place].astype(F32)
            part = mixed_in[c, g].astype(F32) * (gate / (1.0 + jnp.exp(-gate)))
            squares = squares + jnp.sum(part * part, axis=1, keepdims=True)
            gated.append(part)
        inverse = lax.rsqrt(squares * (1.0 / 1024.0) + EPSILON)
        for c in range(CHUNKS):
            place = pl.ds(pl.multiple_of(g * 1024 + c * WIDTH, WIDTH), WIDTH)
            out_ref[:, place] = (gated[c] * inverse * gain_ref[:, place]).astype(BF16)
        return carry

    lax.fori_loop(0, GROUPS, finish, 0)

    arrived(meta, N_DP - 1, send_sem.at[0])
    arrived(writes, N_DP - 1, send_sem.at[1])
    arrived(reads, N_DP - 1, send_sem.at[2])
    arrived(aux_in, N_CTX - 1, send_sem.at[3])
    for c in range(CHUNKS):
        arrived(xs.at[c], N_DP - 1, x_send.at[c])
        arrived(sums_in.at[c], N_CTX - 1, s_send.at[c])
        arrived(states_in.at[c], N_CTX - 1, h_send.at[c])
        arrived(mixed_in.at[c], N_DP - 1, y_send.at[c])


def shards(
    ssm_input,
    gate_input,
    write_basis,
    read_basis,
    step_size,
    decay_rate,
    skip_weight,
    norm_gain,
    row_owner,
    document_lengths,
):
    steps = step_size.astype(F32).T.reshape(GROUPS, HEADS, ROWS)
    owners = row_owner.astype(F32).reshape(1, 1, ROWS)
    lengths = jnp.pad(document_lengths.astype(F32), ((0, 0), (0, ROWS - DOCS))).reshape(1, 1, ROWS)
    packet = jnp.concatenate(
        [
            steps,
            jnp.broadcast_to(owners, (GROUPS, 1, ROWS)),
            jnp.broadcast_to(lengths, (GROUPS, 1, ROWS)),
            jnp.zeros((GROUPS, 6, ROWS), F32),
        ],
        axis=1,
    )
    rates = decay_rate.reshape(GROUPS, HEADS)
    skips = jnp.repeat(skip_weight, 64).reshape(GROUPS, 1024)
    gains = norm_gain.reshape(1, -1)
    hbm = pl.BlockSpec(memory_space=pl.ANY)
    vmem = pl.BlockSpec(memory_space=pltpu.VMEM)
    dma = pltpu.SemaphoreType.DMA
    return pl.pallas_call(
        kernel,
        out_shape=jax.ShapeDtypeStruct((ROWS, GROUPS * 1024), BF16),
        in_specs=[hbm, hbm, hbm, hbm, hbm, vmem, vmem, vmem],
        out_specs=vmem,
        scratch_shapes=[
            pltpu.VMEM((ROWS, GROUPS * 1024), BF16),
            pltpu.VMEM((N_DP, 24, ROWS), F32),
            pltpu.VMEM((N_DP, ROWS, STATE), BF16),
            pltpu.VMEM((N_DP, ROWS, STATE), BF16),
            pltpu.VMEM((CHUNKS, N_DP, ROWS, WIDTH), BF16),
            pltpu.VMEM((N_DP, 8, 1024), F32),
            pltpu.VMEM((N_CTX, 8, 1024), F32),
            pltpu.VMEM((CHUNKS, N_CTX, 64, WIDTH), BF16),
            pltpu.VMEM((CHUNKS, N_CTX, 64, WIDTH), BF16),
            pltpu.VMEM((CHUNKS, N_CTX, 64, WIDTH), BF16),
            pltpu.VMEM((CHUNKS, N_CTX, 64, WIDTH), BF16),
            pltpu.VMEM((CHUNKS, N_DP, ROWS, WIDTH), BF16),
            pltpu.VMEM((CHUNKS, N_DP, ROWS, WIDTH), BF16),
            pltpu.VMEM((N_DP, ROWS, N_DP * ROWS), BF16),
            pltpu.VMEM((CHUNKS, N_DP * ROWS, WIDTH), BF16),
            pltpu.VMEM((N_DP, STATE, N_DP * ROWS), BF16),
            pltpu.VMEM((N_DP, ROWS, N_DP * STATE), BF16),
            pltpu.VMEM((N_DP, ROWS, 128), BF16),
            pltpu.VMEM((N_DP, ROWS), F32),
            pltpu.VMEM((N_DP, ROWS, 128), F32),
            pltpu.VMEM((2, CHUNKS, 128, WIDTH), BF16),
            dma((4 + CHUNKS,)),
            dma((4,)),
            dma((4,)),
            dma((CHUNKS,)),
            dma((CHUNKS,)),
            dma((CHUNKS,)),
            dma((CHUNKS,)),
            dma((CHUNKS,)),
            dma((CHUNKS,)),
            dma((CHUNKS,)),
            dma((CHUNKS,)),
        ],
        compiler_params=pltpu.CompilerParams(
            collective_id=0, has_side_effects=True, vmem_limit_bytes=60 * 2**20
        ),
        cost_estimate=pl.CostEstimate(
            flops=14 * 10**9, bytes_accessed=16 * 2**20, transcendentals=4 * 10**6
        ),
    )(ssm_input, gate_input, write_basis, read_basis, packet, rates, skips, gains)


def solution(mesh):
    placed = (
        P(("dp", "ctx"), None),
        P(("dp", "ctx"), None),
        P(("dp", "ctx"), None),
        P(("dp", "ctx"), None),
        P(("dp", "ctx"), None),
        P(),
        P(),
        P(),
        P(("dp", "ctx"), None),
        P("dp", None),
    )
    return jax.shard_map(
        shards, mesh=mesh, in_specs=placed, out_specs=P(("dp", "ctx"), None), check_vma=False
    )
```

```python
import jax
import jax.numpy as jnp
from jax import lax
from jax.experimental import pallas as pl
from jax.experimental.pallas import tpu as pltpu
from jax.sharding import PartitionSpec as P

GROUPS = 8
BLOCK = 512
EPSILON = 1e-05
CHUNKS = 4
N_DP = 8
N_CTX = 16
ROWS = 256
HEADS = 16
WIDTH = 1024 // CHUNKS
STATE = 128
DOCS = 8
SLOTS = 64
MESH = pl.DeviceIdType.MESH
F32 = jnp.float32
BF16 = jnp.bfloat16


def dot(a, b, dims=((1,), (0,)), precision=None):
    return lax.dot_general(a, b, (dims, ((), ())), precision=precision, preferred_element_type=F32)


def exact(a, b, dims=((1,), (0,))):
    return dot(a, b, dims, lax.Precision.HIGHEST)


def thirds(value):
    high = value.astype(BF16).astype(F32)
    middle = (value - high).astype(BF16).astype(F32)
    low = (value - high - middle).astype(BF16).astype(F32)
    return high, middle, low


def iota(shape, dim):
    return lax.broadcasted_iota(jnp.int32, shape, dim)


def kernel(
    x_ref,
    write_ref,
    read_ref,
    step_ref,
    owner_hbm,
    length_hbm,
    rate_hbm,
    skip_hbm,
    out_ref,
    owner_ref,
    length_ref,
    rate_ref,
    skip_ref,
    steps,
    packet,
    skips,
    meta,
    writes,
    reads,
    xs,
    aux,
    aux_in,
    sums,
    sums_in,
    states,
    states_in,
    mixed,
    scores,
    scaled,
    writes_t,
    reads_m,
    factors,
    keys_row,
    keys_col,
    spread,
    small_sem,
    local_sem,
    send_sem,
    recv_sem,
    x_send,
    x_recv,
    s_send,
    s_recv,
    h_send,
    h_recv,
    y_send,
    y_recv,
):
    me = lax.axis_index("dp")
    col = lax.axis_index("ctx")

    def remote(src, dst, send, recv, axis, peer):
        return pltpu.make_async_remote_copy(
            src_ref=src,
            dst_ref=dst,
            send_sem=send,
            recv_sem=recv,
            device_id={axis: peer},
            device_id_type=MESH,
        )

    def lanes(ref, start, width):
        return ref.at[:, pl.ds(pl.multiple_of(start, 128), width)]

    def piece(ref, owner, c):
        return lanes(ref, owner * 1024 + c * WIDTH, WIDTH)

    barrier = pltpu.get_barrier_semaphore()
    for d in range(1, N_DP):
        pl.semaphore_signal(
            barrier, inc=1, device_id={"dp": lax.rem(me + d, N_DP)}, device_id_type=MESH
        )
    for d in range(1, N_CTX):
        pl.semaphore_signal(
            barrier, inc=1, device_id={"ctx": lax.rem(col + d, N_CTX)}, device_id_type=MESH
        )

    own = [
        pltpu.make_async_copy(step_ref, steps, local_sem.at[0]),
        pltpu.make_async_copy(lanes(write_ref, me * STATE, STATE), writes.at[me], local_sem.at[1]),
        pltpu.make_async_copy(lanes(read_ref, me * STATE, STATE), reads.at[me], local_sem.at[2]),
    ]
    own_x = [
        pltpu.make_async_copy(piece(x_ref, me, c), xs.at[c, me], local_sem.at[4 + c])
        for c in range(CHUNKS)
    ]
    small = [
        pltpu.make_async_copy(owner_hbm, owner_ref, small_sem.at[0]),
        pltpu.make_async_copy(length_hbm, length_ref, small_sem.at[1]),
        pltpu.make_async_copy(rate_hbm, rate_ref, small_sem.at[2]),
        pltpu.make_async_copy(skip_hbm, skip_ref, small_sem.at[3]),
    ]
    for copy in own[:1] + small + own[1:] + own_x:
        copy.start()
    pl.semaphore_wait(barrier, N_DP + N_CTX - 2)

    for d in range(1, N_DP):
        peer = lax.rem(me + d, N_DP)
        remote(
            lanes(write_ref, peer * STATE, STATE),
            writes.at[me],
            send_sem.at[1],
            recv_sem.at[1],
            "dp",
            peer,
        ).start()
        remote(
            lanes(read_ref, peer * STATE, STATE),
            reads.at[me],
            send_sem.at[2],
            recv_sem.at[2],
            "dp",
            peer,
        ).start()

    own[0].wait()
    for copy in small:
        copy.wait()
    packet[:, 0:HEADS, :] = steps[...].astype(F32).T.reshape(GROUPS, HEADS, ROWS).astype(BF16)
    owner_row = owner_ref[...].astype(F32)
    line = iota((16, ROWS), 0)
    lane = iota((16, ROWS), 1)
    extra = jnp.where(line == 0, owner_row, 0.0)
    for d in range(DOCS):
        length = length_ref[0:1, d : d + 1]
        extra = jnp.where((line == 1) & (lane == d), (length // 64).astype(F32), extra)
        extra = jnp.where((line == 2) & (lane == d), (length % 64).astype(F32), extra)
    for k in range(GROUPS):
        packet[k, 16:32, :] = extra.astype(BF16)
    for d in range(1, N_DP):
        peer = lax.rem(me + d, N_DP)
        remote(
            packet.at[peer], meta.at[me], send_sem.at[0], recv_sem.at[0], "dp", peer
        ).start()
    meta[me] = packet[me]
    for c in range(CHUNKS):
        for d in range(1, N_DP):
            peer = lax.rem(me + d, N_DP)
            remote(
                piece(x_ref, peer, c), xs.at[c, me], x_send.at[c], x_recv.at[c], "dp", peer
            ).start()

    row = iota((128, WIDTH), 0)
    for c in range(CHUNKS):
        head = c * (HEADS // CHUNKS) + iota((128, WIDTH), 1) // 64
        named = lax.rem(row, HEADS) == head
        spread[0, c] = jnp.where(named & (row < 48), 1.0, 0.0).astype(BF16)
        spread[1, c] = jnp.where(named & (row >= 48) & (row < 96), 1.0, 0.0).astype(BF16)
        mine = jnp.where(row == me * HEADS + head, 1.0, 0.0)
        skips[c] = exact(jnp.broadcast_to(skip_ref[...], (8, 128)), mine)

    def arrived(ref, count, sem):
        part = ref.at[pl.ds(0, count)]
        pltpu.make_async_copy(part, part, sem).wait()

    arrived(meta, N_DP - 1, recv_sem.at[0])
    first_slot = (col * BLOCK).astype(F32)

    extras = meta[:, 16:32, :].astype(F32)
    owners = extras[:, 0, :]
    lengths = extras[:, 1, :] * 64.0 + extras[:, 2, :]
    starts = []
    total = jnp.zeros((N_DP, 1), F32)
    for d in range(DOCS):
        starts.append(total)
        total = total + lengths[:, d : d + 1]
    sequence = iota((N_DP, 1), 0).astype(F32)
    table = jnp.where(
        owners[:, None, :] == iota((N_DP, N_DP, ROWS), 1).astype(F32), 1.0, 0.0
    )
    earlier = jnp.where(iota((ROWS, ROWS), 0) < iota((ROWS, ROWS), 1), 1.0, 0.0)
    counts = dot(table.reshape(N_DP * N_DP, ROWS).astype(BF16), earlier.astype(BF16))
    rank = jnp.sum(table * counts.reshape(N_DP, N_DP, ROWS), axis=1)
    slot = first_slot + (iota((N_DP, ROWS), 0) * SLOTS).astype(F32) + rank
    segment = jnp.zeros((N_DP, N_DP, ROWS), F32)
    before = jnp.zeros((N_DP, 1), F32)
    end = jnp.zeros((N_DP, 1), F32)
    for d in range(DOCS):
        segment = segment + jnp.where(slot[:, None, :] >= starts[d][None], 1.0, 0.0)
        before = before + jnp.where(first_slot - 1.0 >= starts[d], 1.0, 0.0)
        end = end + jnp.where(first_slot + (BLOCK - 1.0) >= starts[d], 1.0, 0.0)
    key = owners * 16.0 + jnp.sum(table * segment, axis=1)
    key_before = sequence * 16.0 + before
    key_end = sequence * 16.0 + end
    same_document = jnp.where(key_before == key_end, 1.0, 0.0)
    keys_row[...] = key
    key_t = key.T
    owner_t = owners.T

    rate = jnp.sum(
        jnp.where(
            iota((HEADS, 128), 1) == iota((HEADS, 128), 0) + me * HEADS, rate_ref[...], 0.0
        ),
        axis=1,
        keepdims=True,
    )
    rate_row = jnp.sum(
        jnp.where(iota((HEADS, HEADS), 0) == iota((HEADS, HEADS), 1), rate, 0.0),
        axis=0,
        keepdims=True,
    )
    not_later = iota((ROWS, ROWS), 0) <= iota((ROWS, ROWS), 1)
    sofar = jnp.zeros((HEADS, N_DP), F32)
    whole_t = jnp.zeros((N_DP, HEADS), F32)
    running = []
    for i in range(N_DP):
        keys_col[i] = jnp.broadcast_to(key_t[:, i : i + 1], (ROWS, 128))
        step = meta[i, 0:HEADS, :]
        owned = table[i]
        same = jnp.where((owner_t[:, i : i + 1] == owners[i : i + 1, :]) & not_later, 1.0, 0.0)
        running.append(dot(step, same.astype(BF16)) + exact(sofar, owned))
        sofar = sofar + dot(step, owned.astype(BF16), ((1,), (1,)))
        whole_t = whole_t + dot(owned.astype(BF16), step, ((1,), (1,)))
    middle = -0.5 * rate * sofar
    for i in range(N_DP):
        exponent = -rate * running[i] - exact(middle, table[i])
        rising = thirds(jnp.exp(-exponent) * meta[i, 0:HEADS, :].astype(F32))
        falling = thirds(jnp.exp(exponent))
        stack = jnp.concatenate(falling + rising + (jnp.zeros((32, ROWS), F32),), axis=0)
        factors[i] = stack.T.astype(BF16)
    middle_t = -0.5 * whole_t * rate_row
    half_decay = thirds(jnp.exp(middle_t))
    full_decay = thirds(jnp.exp(2.0 * middle_t) * same_document)
    for c in range(CHUNKS):
        heads = spread[0, c, 0:HEADS, :]
        half = sum(dot(part.astype(BF16), heads) for part in half_decay)
        full = sum(dot(part.astype(BF16), heads) for part in full_decay)
        for k in range(N_DP):
            aux[k, 0:1, c * WIDTH : (c + 1) * WIDTH] = full[k : k + 1, :]
            aux[k, 1:2, c * WIDTH : (c + 1) * WIDTH] = half[k : k + 1, :]
    for k in range(N_DP):
        aux[k, 2:8, :] = jnp.zeros((6, 1024), F32)
    for d in range(1, N_CTX):
        peer = lax.rem(col + d, N_CTX)
        remote(
            aux.at[peer // 2], aux_in.at[col], send_sem.at[3], recv_sem.at[3], "ctx", peer
        ).start()
    aux_in[col] = aux[col // 2]

    own[1].wait()
    arrived(writes, N_DP - 1, recv_sem.at[1])
    for i in range(N_DP):
        flipped = writes[i].astype(F32).T
        for k in range(N_DP):
            kept = keys_row[i : i + 1, :] == key_end[k : k + 1, :]
            writes_t[k, :, i * ROWS : (i + 1) * ROWS] = jnp.where(kept, flipped, 0.0).astype(BF16)
    own[2].wait()
    arrived(reads, N_DP - 1, recv_sem.at[2])

    for i in range(N_DP):
        block = reads[i].astype(F32)
        for k in range(N_DP):
            kept = keys_col[i] == key_before[k : k + 1, :]
            reads_m[i, :, k * STATE : (k + 1) * STATE] = jnp.where(kept, block, 0.0).astype(BF16)

    ordered = iota((ROWS, ROWS), 0) >= iota((ROWS, ROWS), 1)

    def score_rows(i, carry):
        key_q = keys_col[i][:, 0:1]
        block = reads[i]

        def score(j, carry):
            raw = dot(block, writes[j], ((1,), (1,)))
            kept = (key_q == keys_row[pl.ds(j, 1), :]) & (ordered | (j < i))
            scores[i, :, pl.ds(pl.multiple_of(j * ROWS, ROWS), ROWS)] = jnp.where(
                kept, raw, 0.0
            ).astype(BF16)
            return carry

        return lax.fori_loop(0, i + 1, score, carry)

    lax.fori_loop(0, N_DP, score_rows, 0)

    def summarize(c):
        pltpu.make_async_copy(xs.at[0, 0], xs.at[0, 0], local_sem.at[4 + c]).wait()
        arrived(xs.at[c], N_DP - 1, x_recv.at[c])

        def scale(i, carry):
            factor = dot(factors[i], spread[1, c])
            scaled[c, pl.ds(pl.multiple_of(i * ROWS, ROWS), ROWS), :] = (
                xs[c, i].astype(F32) * factor
            ).astype(BF16)
            return carry

        lax.fori_loop(0, N_DP, scale, 0)

        def collect(k, carry):
            k = lax.rem(k + col // 2, N_DP)
            part = dot(writes_t[k], scaled[c])
            half = aux[k, 1:2, pl.ds(pl.multiple_of(c * WIDTH, WIDTH), WIDTH)]
            part = (part * half).astype(BF16)
            for side in range(2):
                peer = 2 * k + side
                sums[c, peer] = part[64 * side : 64 * side + 64]

                @pl.when(peer != col)
                def _():
                    remote(
                        sums.at[c, peer], sums_in.at[c, col], s_send.at[c], s_recv.at[c], "ctx", peer
                    ).start()

            return carry

        lax.fori_loop(0, N_DP, collect, 0)
        sums_in[c, col] = sums[c, col]

    def carry_on(c):
        @pl.when(c == 0)
        def _():
            arrived(aux_in, N_CTX - 1, recv_sem.at[3])

        arrived(sums_in.at[c], N_CTX - 1, s_recv.at[c])
        window = pl.ds(pl.multiple_of(c * WIDTH, WIDTH), WIDTH)

        def advance(j, held):
            states[c, j] = (held * aux_in[j, 1:2, window]).astype(BF16)
            return held * aux_in[j, 0:1, window] + sums_in[c, j].astype(F32)

        lax.fori_loop(0, N_CTX, advance, jnp.zeros((64, WIDTH), F32))
        for d in range(1, N_CTX):
            peer = lax.rem(col + d, N_CTX)
            remote(
                states.at[c, peer], states_in.at[c, col], h_send.at[c], h_recv.at[c], "ctx", peer
            ).start()
        states_in[c, col] = states[c, col]

    def hand_back(c, peer):
        remote(
            mixed.at[c, peer], piece(out_ref, me, c), y_send.at[c], y_recv.at[c], "dp", peer
        ).start()

    def mix(c):
        arrived(states_in.at[c], N_CTX - 1, h_recv.at[c])

        carried = states_in[c].reshape(N_DP * STATE, WIDTH)
        skip = skips[c, 0:1, :]
        for i in range(N_DP):
            reach = (i + 1) * ROWS
            both = dot(scores[i, :, 0:reach], scaled[c, 0:reach, :]) + dot(reads_m[i], carried)
            factor = dot(factors[i], spread[0, c])
            mixed[c, i] = (both * factor + skip * xs[c, i].astype(F32)).astype(BF16)

            @pl.when(me != i)
            def _():
                hand_back(c, i)

        pltpu.make_async_copy(mixed.at[c, me], piece(out_ref, me, c), local_sem.at[3]).start()

    def step(s, carry):
        @pl.when(s < CHUNKS)
        def _():
            summarize(s)

        @pl.when((s > 0) & (s < CHUNKS + 1))
        def _():
            carry_on(s - 1)

        @pl.when(s > 1)
        def _():
            mix(s - 2)

        return carry

    lax.fori_loop(0, CHUNKS + 2, step, 0)

    arrived(mixed.at[0], CHUNKS, local_sem.at[3])
    for c in range(CHUNKS):
        arrived(mixed.at[c], N_DP - 1, y_recv.at[c])

    arrived(meta, N_DP - 1, send_sem.at[0])
    arrived(writes, N_DP - 1, send_sem.at[1])
    arrived(reads, N_DP - 1, send_sem.at[2])
    arrived(aux_in, N_CTX - 1, send_sem.at[3])
    for c in range(CHUNKS):
        arrived(xs.at[c], N_DP - 1, x_send.at[c])
        arrived(sums_in.at[c], N_CTX - 1, s_send.at[c])
        arrived(states_in.at[c], N_CTX - 1, h_send.at[c])
        arrived(mixed.at[c], N_DP - 1, y_send.at[c])


def finish(mixed_hbm, gate_hbm, gain_ref, out_ref, mixed, gates, done, load_sem, done_sem):
    def part(ref, g):
        return ref.at[:, pl.ds(pl.multiple_of(g * 1024, 1024), 1024)]

    for g in range(GROUPS):
        pltpu.make_async_copy(part(gate_hbm, g), gates.at[g], load_sem.at[0, g]).start()
        pltpu.make_async_copy(part(mixed_hbm, g), mixed.at[g], load_sem.at[1, g]).start()

    def group(g, carry):
        pltpu.make_async_copy(part(gate_hbm, g), gates.at[g], load_sem.at[0, g]).wait()
        pltpu.make_async_copy(part(mixed_hbm, g), mixed.at[g], load_sem.at[1, g]).wait()
        gate = gates[g].astype(F32)
        gated = mixed[g].astype(F32) * (gate / (1.0 + jnp.exp(-gate)))
        inverse = lax.rsqrt(jnp.mean(gated * gated, axis=1, keepdims=True) + EPSILON)
        gain = gain_ref[:, pl.ds(pl.multiple_of(g * 1024, 1024), 1024)]
        done[g] = (gated * inverse * gain).astype(BF16)
        pltpu.make_async_copy(done.at[g], part(out_ref, g), done_sem.at[g]).start()
        return carry

    lax.fori_loop(0, GROUPS, group, 0)
    for g in range(GROUPS):
        pltpu.make_async_copy(done.at[g], part(out_ref, g), done_sem.at[g]).wait()


def shards(
    ssm_input,
    gate_input,
    write_basis,
    read_basis,
    step_size,
    decay_rate,
    skip_weight,
    norm_gain,
    row_owner,
    document_lengths,
):
    hbm = pl.BlockSpec(memory_space=pltpu.HBM)
    anywhere = pl.BlockSpec(memory_space=pl.ANY)
    vmem = pl.BlockSpec(memory_space=pltpu.VMEM)
    dma = pltpu.SemaphoreType.DMA
    mixed = pl.pallas_call(
        kernel,
        out_shape=jax.ShapeDtypeStruct((ROWS, GROUPS * 1024), BF16),
        in_specs=[hbm] * 8,
        out_specs=anywhere,
        scratch_shapes=[
            pltpu.VMEM((1, ROWS), jnp.int32),
            pltpu.VMEM((1, DOCS), jnp.int32),
            pltpu.VMEM((1, 128), F32),
            pltpu.VMEM((1, 128), F32),
            pltpu.VMEM((ROWS, 128), BF16),
            pltpu.VMEM((N_DP, 32, ROWS), BF16),
            pltpu.VMEM((CHUNKS, 8, WIDTH), F32),
            pltpu.VMEM((N_DP, 32, ROWS), BF16),
            pltpu.VMEM((N_DP, ROWS, STATE), BF16),
            pltpu.VMEM((N_DP, ROWS, STATE), BF16),
            pltpu.VMEM((CHUNKS, N_DP, ROWS, WIDTH), BF16),
            pltpu.VMEM((N_DP, 8, 1024), F32),
            pltpu.VMEM((N_CTX, 8, 1024), F32),
            pltpu.VMEM((CHUNKS, N_CTX, 64, WIDTH), BF16),
            pltpu.VMEM((CHUNKS, N_CTX, 64, WIDTH), BF16),
            pltpu.VMEM((CHUNKS, N_CTX, 64, WIDTH), BF16),
            pltpu.VMEM((CHUNKS, N_CTX, 64, WIDTH), BF16),
            pltpu.VMEM((CHUNKS, N_DP, ROWS, WIDTH), BF16),
            pltpu.VMEM((N_DP, ROWS, N_DP * ROWS), BF16),
            pltpu.VMEM((CHUNKS, N_DP * ROWS, WIDTH), BF16),
            pltpu.VMEM((N_DP, STATE, N_DP * ROWS), BF16),
            pltpu.VMEM((N_DP, ROWS, N_DP * STATE), BF16),
            pltpu.VMEM((N_DP, ROWS, 128), BF16),
            pltpu.VMEM((N_DP, ROWS), F32),
            pltpu.VMEM((N_DP, ROWS, 128), F32),
            pltpu.VMEM((2, CHUNKS, 128, WIDTH), BF16),
            dma((4,)),
            dma((4 + CHUNKS,)),
            dma((4,)),
            dma((4,)),
            dma((CHUNKS,)),
            dma((CHUNKS,)),
            dma((CHUNKS,)),
            dma((CHUNKS,)),
            dma((CHUNKS,)),
            dma((CHUNKS,)),
            dma((CHUNKS,)),
            dma((CHUNKS,)),
        ],
        compiler_params=pltpu.CompilerParams(
            collective_id=0, has_side_effects=True, vmem_limit_bytes=54 * 2**20
        ),
        cost_estimate=pl.CostEstimate(
            flops=14 * 10**9, bytes_accessed=16 * 2**20, transcendentals=4 * 10**6
        ),
    )(
        ssm_input,
        write_basis,
        read_basis,
        step_size,
        row_owner.reshape(1, -1),
        document_lengths,
        decay_rate.reshape(1, -1),
        skip_weight.reshape(1, -1),
    )
    return pl.pallas_call(
        finish,
        out_shape=jax.ShapeDtypeStruct((ROWS, GROUPS * 1024), BF16),
        in_specs=[anywhere, anywhere, vmem],
        out_specs=anywhere,
        scratch_shapes=[
            pltpu.VMEM((GROUPS, ROWS, 1024), BF16),
            pltpu.VMEM((GROUPS, ROWS, 1024), BF16),
            pltpu.VMEM((GROUPS, ROWS, 1024), BF16),
            dma((2, GROUPS)),
            dma((GROUPS,)),
        ],
        compiler_params=pltpu.CompilerParams(vmem_limit_bytes=54 * 2**20),
        cost_estimate=pl.CostEstimate(
            flops=20 * 2**20, bytes_accessed=12 * 2**20, transcendentals=2 * 2**20
        ),
    )(mixed, gate_input, norm_gain.reshape(1, -1))


def solution(mesh):
    placed = (
        P(("dp", "ctx"), None),
        P(("dp", "ctx"), None),
        P(("dp", "ctx"), None),
        P(("dp", "ctx"), None),
        P(("dp", "ctx"), None),
        P(),
        P(),
        P(),
        P(("dp", "ctx"), None),
        P("dp", None),
    )
    return jax.shard_map(
        shards, mesh=mesh, in_specs=placed, out_specs=P(("dp", "ctx"), None), check_vma=False
    )
```

```python
import jax
import jax.numpy as jnp
from jax import lax
from jax.experimental import pallas as pl
from jax.experimental.pallas import tpu as pltpu
from jax.sharding import PartitionSpec as P

GROUPS = 8
BLOCK = 512
EPSILON = 1e-05
CHUNKS = 4
N_DP = 8
N_CTX = 16
ROWS = 256
HEADS = 16
WIDTH = 1024 // CHUNKS
STATE = 128
DOCS = 8
SLOTS = 64
MESH = pl.DeviceIdType.MESH
F32 = jnp.float32
BF16 = jnp.bfloat16


def dot(a, b, dims=((1,), (0,)), precision=None):
    return lax.dot_general(a, b, (dims, ((), ())), precision=precision, preferred_element_type=F32)


def exact(a, b, dims=((1,), (0,))):
    return dot(a, b, dims, lax.Precision.HIGHEST)


def thirds(value):
    high = value.astype(BF16).astype(F32)
    middle = (value - high).astype(BF16).astype(F32)
    low = (value - high - middle).astype(BF16).astype(F32)
    return high, middle, low


def silu(value):
    return value / (1.0 + jnp.exp(-value))


def iota(shape, dim):
    return lax.broadcasted_iota(jnp.int32, shape, dim)


def kernel(
    x_ref,
    write_ref,
    read_ref,
    step_ref,
    owner_hbm,
    length_hbm,
    rate_hbm,
    skip_hbm,
    gate_hbm,
    gated_ref,
    squares_ref,
    last_ref,
    gates,
    landed,
    squares,
    owner_ref,
    length_ref,
    rate_ref,
    skip_ref,
    steps,
    packet,
    skips,
    meta,
    writes,
    reads,
    xs,
    aux,
    aux_in,
    sums,
    sums_in,
    states,
    states_in,
    mixed,
    scores,
    scaled,
    writes_t,
    reads_m,
    factors,
    keys_row,
    keys_col,
    spread,
    inner,
    gate_sem,
    done_sem,
    small_sem,
    local_sem,
    send_sem,
    recv_sem,
    x_send,
    x_recv,
    s_send,
    s_recv,
    h_send,
    h_recv,
    y_send,
    y_recv,
):
    me = lax.axis_index("dp")
    col = lax.axis_index("ctx")

    def remote(src, dst, send, recv, axis, peer):
        return pltpu.make_async_remote_copy(
            src_ref=src,
            dst_ref=dst,
            send_sem=send,
            recv_sem=recv,
            device_id={axis: peer},
            device_id_type=MESH,
        )

    def lanes(ref, start, width):
        return ref.at[:, pl.ds(pl.multiple_of(start, 128), width)]

    def piece(ref, owner, c):
        return lanes(ref, owner * 1024 + c * WIDTH, WIDTH)

    barrier = pltpu.get_barrier_semaphore()
    for d in range(1, N_DP):
        pl.semaphore_signal(
            barrier, inc=1, device_id={"dp": lax.rem(me + d, N_DP)}, device_id_type=MESH
        )
    for d in range(1, N_CTX):
        pl.semaphore_signal(
            barrier, inc=1, device_id={"ctx": lax.rem(col + d, N_CTX)}, device_id_type=MESH
        )

    own = [
        pltpu.make_async_copy(step_ref, steps, local_sem.at[0]),
        pltpu.make_async_copy(lanes(write_ref, me * STATE, STATE), writes.at[me], local_sem.at[1]),
        pltpu.make_async_copy(lanes(read_ref, me * STATE, STATE), reads.at[me], local_sem.at[2]),
    ]
    own_x = [
        pltpu.make_async_copy(piece(x_ref, me, c), xs.at[c, me], local_sem.at[4 + c])
        for c in range(CHUNKS)
    ]
    small = [
        pltpu.make_async_copy(owner_hbm, owner_ref, small_sem.at[0]),
        pltpu.make_async_copy(length_hbm, length_ref, small_sem.at[1]),
        pltpu.make_async_copy(rate_hbm, rate_ref, small_sem.at[2]),
        pltpu.make_async_copy(skip_hbm, skip_ref, small_sem.at[3]),
    ]
    gate_copy = pltpu.make_async_copy(gate_hbm, gates, gate_sem.at[0])
    for copy in own[:1] + small + own[1:] + own_x + [gate_copy]:
        copy.start()
    pl.semaphore_wait(barrier, N_DP + N_CTX - 2)

    for d in range(1, N_DP):
        peer = lax.rem(me + d, N_DP)
        remote(
            lanes(write_ref, peer * STATE, STATE),
            writes.at[me],
            send_sem.at[1],
            recv_sem.at[1],
            "dp",
            peer,
        ).start()
        remote(
            lanes(read_ref, peer * STATE, STATE),
            reads.at[me],
            send_sem.at[2],
            recv_sem.at[2],
            "dp",
            peer,
        ).start()

    own[0].wait()
    for copy in small:
        copy.wait()
    packet[:, 0:HEADS, :] = steps[...].astype(F32).T.reshape(GROUPS, HEADS, ROWS).astype(BF16)
    owner_row = owner_ref[...].astype(F32)
    line = iota((16, ROWS), 0)
    lane = iota((16, ROWS), 1)
    extra = jnp.where(line == 0, owner_row, 0.0)
    for d in range(DOCS):
        length = length_ref[0:1, d : d + 1]
        extra = jnp.where((line == 1) & (lane == d), (length // 64).astype(F32), extra)
        extra = jnp.where((line == 2) & (lane == d), (length % 64).astype(F32), extra)
    for k in range(GROUPS):
        packet[k, 16:32, :] = extra.astype(BF16)
    for d in range(1, N_DP):
        peer = lax.rem(me + d, N_DP)
        remote(
            packet.at[peer], meta.at[me], send_sem.at[0], recv_sem.at[0], "dp", peer
        ).start()
    meta[me] = packet[me]
    for c in range(CHUNKS):
        for d in range(1, N_DP):
            peer = lax.rem(me + d, N_DP)
            remote(
                piece(x_ref, peer, c), xs.at[c, me], x_send.at[c], x_recv.at[c], "dp", peer
            ).start()

    row = iota((128, WIDTH), 0)
    for c in range(CHUNKS):
        head = c * (HEADS // CHUNKS) + iota((128, WIDTH), 1) // 64
        named = lax.rem(row, HEADS) == head
        spread[0, c] = jnp.where(named & (row < 48), 1.0, 0.0).astype(BF16)
        spread[1, c] = jnp.where(named & (row >= 48) & (row < 96), 1.0, 0.0).astype(BF16)
        mine = jnp.where(row == me * HEADS + head, 1.0, 0.0)
        skips[c] = exact(jnp.broadcast_to(skip_ref[...], (8, 128)), mine)

    def arrived(ref, count, sem):
        part = ref.at[pl.ds(0, count)]
        pltpu.make_async_copy(part, part, sem).wait()

    arrived(meta, N_DP - 1, recv_sem.at[0])
    first_slot = (col * BLOCK).astype(F32)

    extras = meta[:, 16:32, :].astype(F32)
    owners = extras[:, 0, :]
    lengths = extras[:, 1, :] * 64.0 + extras[:, 2, :]
    starts = []
    total = jnp.zeros((N_DP, 1), F32)
    for d in range(DOCS):
        starts.append(total)
        total = total + lengths[:, d : d + 1]
    sequence = iota((N_DP, 1), 0).astype(F32)
    table = jnp.where(
        owners[:, None, :] == iota((N_DP, N_DP, ROWS), 1).astype(F32), 1.0, 0.0
    )
    earlier = jnp.where(iota((ROWS, ROWS), 0) < iota((ROWS, ROWS), 1), 1.0, 0.0)
    counts = dot(table.reshape(N_DP * N_DP, ROWS).astype(BF16), earlier.astype(BF16))
    rank = jnp.sum(table * counts.reshape(N_DP, N_DP, ROWS), axis=1)
    slot = first_slot + (iota((N_DP, ROWS), 0) * SLOTS).astype(F32) + rank
    segment = jnp.zeros((N_DP, N_DP, ROWS), F32)
    before = jnp.zeros((N_DP, 1), F32)
    end = jnp.zeros((N_DP, 1), F32)
    for d in range(DOCS):
        segment = segment + jnp.where(slot[:, None, :] >= starts[d][None], 1.0, 0.0)
        before = before + jnp.where(first_slot - 1.0 >= starts[d], 1.0, 0.0)
        end = end + jnp.where(first_slot + (BLOCK - 1.0) >= starts[d], 1.0, 0.0)
    key = owners * 16.0 + jnp.sum(table * segment, axis=1)
    key_before = sequence * 16.0 + before
    key_end = sequence * 16.0 + end
    same_document = jnp.where(key_before == key_end, 1.0, 0.0)
    keys_row[...] = key
    key_t = key.T
    owner_t = owners.T

    rate = jnp.sum(
        jnp.where(
            iota((HEADS, 128), 1) == iota((HEADS, 128), 0) + me * HEADS, rate_ref[...], 0.0
        ),
        axis=1,
        keepdims=True,
    )
    rate_row = jnp.sum(
        jnp.where(iota((HEADS, HEADS), 0) == iota((HEADS, HEADS), 1), rate, 0.0),
        axis=0,
        keepdims=True,
    )
    not_later = iota((ROWS, ROWS), 0) <= iota((ROWS, ROWS), 1)
    sofar = jnp.zeros((HEADS, N_DP), F32)
    whole_t = jnp.zeros((N_DP, HEADS), F32)
    running = []
    for i in range(N_DP):
        keys_col[i] = jnp.broadcast_to(key_t[:, i : i + 1], (ROWS, 128))
        step = meta[i, 0:HEADS, :]
        owned = table[i]
        same = jnp.where((owner_t[:, i : i + 1] == owners[i : i + 1, :]) & not_later, 1.0, 0.0)
        running.append(dot(step, same.astype(BF16)) + exact(sofar, owned))
        sofar = sofar + dot(step, owned.astype(BF16), ((1,), (1,)))
        whole_t = whole_t + dot(owned.astype(BF16), step, ((1,), (1,)))
    middle = -0.5 * rate * sofar
    for i in range(N_DP):
        exponent = -rate * running[i] - exact(middle, table[i])
        rising = thirds(jnp.exp(-exponent) * meta[i, 0:HEADS, :].astype(F32))
        falling = thirds(jnp.exp(exponent))
        stack = jnp.concatenate(falling + rising + (jnp.zeros((32, ROWS), F32),), axis=0)
        factors[i] = stack.T.astype(BF16)
    middle_t = -0.5 * whole_t * rate_row
    half_decay = thirds(jnp.exp(middle_t))
    full_decay = thirds(jnp.exp(2.0 * middle_t) * same_document)
    for c in range(CHUNKS):
        heads = spread[0, c, 0:HEADS, :]
        half = sum(dot(part.astype(BF16), heads) for part in half_decay)
        full = sum(dot(part.astype(BF16), heads) for part in full_decay)
        for k in range(N_DP):
            aux[k, 0:1, c * WIDTH : (c + 1) * WIDTH] = full[k : k + 1, :]
            aux[k, 1:2, c * WIDTH : (c + 1) * WIDTH] = half[k : k + 1, :]
    for k in range(N_DP):
        aux[k, 2:8, :] = jnp.zeros((6, 1024), F32)
    for d in range(1, N_CTX):
        peer = lax.rem(col + d, N_CTX)
        remote(
            aux.at[peer // 2], aux_in.at[col], send_sem.at[3], recv_sem.at[3], "ctx", peer
        ).start()
    aux_in[col] = aux[col // 2]

    own[1].wait()
    arrived(writes, N_DP - 1, recv_sem.at[1])
    for i in range(N_DP):
        flipped = writes[i].astype(F32).T
        for k in range(N_DP):
            kept = keys_row[i : i + 1, :] == key_end[k : k + 1, :]
            half = pl.ds((k % 2) * STATE, STATE)
            writes_t[k // 2, half, i * ROWS : (i + 1) * ROWS] = jnp.where(
                kept, flipped, 0.0
            ).astype(BF16)
    own[2].wait()
    arrived(reads, N_DP - 1, recv_sem.at[2])

    for i in range(N_DP):
        block = reads[i].astype(F32)
        for k in range(N_DP):
            kept = keys_col[i] == key_before[k : k + 1, :]
            reads_m[i, :, k * STATE : (k + 1) * STATE] = jnp.where(kept, block, 0.0).astype(BF16)

    ordered = iota((ROWS, ROWS), 0) >= iota((ROWS, ROWS), 1)

    def score_rows(i, carry):
        key_q = keys_col[i][:, 0:1]
        block = reads[i]

        def score(j, carry):
            raw = dot(block, writes[j], ((1,), (1,)))
            kept = (key_q == keys_row[pl.ds(j, 1), :]) & (ordered | (j < i))
            scores[i, :, pl.ds(pl.multiple_of(j * ROWS, ROWS), ROWS)] = jnp.where(
                kept, raw, 0.0
            ).astype(BF16)
            return carry

        return lax.fori_loop(0, i + 1, score, carry)

    lax.fori_loop(0, N_DP, score_rows, 0)

    def summarize(c):
        pltpu.make_async_copy(xs.at[0, 0], xs.at[0, 0], local_sem.at[4 + c]).wait()
        arrived(xs.at[c], N_DP - 1, x_recv.at[c])

        def scale(i, carry):
            factor = dot(factors[i], spread[1, c])
            scaled[c, pl.ds(pl.multiple_of(i * ROWS, ROWS), ROWS), :] = (
                xs[c, i].astype(F32) * factor
            ).astype(BF16)
            return carry

        lax.fori_loop(0, N_DP, scale, 0)

        def collect(k, carry):
            pair = lax.rem(k + col // 4, N_DP // 2)
            part = dot(writes_t[pair], scaled[c])
            for side in range(4):
                peer = 4 * pair + side
                half = aux[
                    2 * pair + side // 2, 1:2, pl.ds(pl.multiple_of(c * WIDTH, WIDTH), WIDTH)
                ]
                sums[c, peer] = (part[64 * side : 64 * side + 64] * half).astype(BF16)

                @pl.when(peer != col)
                def _():
                    remote(
                        sums.at[c, peer], sums_in.at[c, col], s_send.at[c], s_recv.at[c], "ctx", peer
                    ).start()

            return carry

        lax.fori_loop(0, N_DP // 2, collect, 0)
        sums_in[c, col] = sums[c, col]

    def carry_on(c):
        @pl.when(c == 0)
        def _():
            arrived(aux_in, N_CTX - 1, recv_sem.at[3])

        arrived(sums_in.at[c], N_CTX - 1, s_recv.at[c])
        window = pl.ds(pl.multiple_of(c * WIDTH, WIDTH), WIDTH)

        def advance(j, held):
            states[c, j] = (held * aux_in[j, 1:2, window]).astype(BF16)
            return held * aux_in[j, 0:1, window] + sums_in[c, j].astype(F32)

        lax.fori_loop(0, N_CTX, advance, jnp.zeros((64, WIDTH), F32))
        for d in range(1, N_CTX):
            peer = lax.rem(col + d, N_CTX)
            remote(
                states.at[c, peer], states_in.at[c, col], h_send.at[c], h_recv.at[c], "ctx", peer
            ).start()
        states_in[c, col] = states[c, col]

    def hand_back(c, peer):
        remote(
            mixed.at[c, peer], piece(out_ref, me, c), y_send.at[c], y_recv.at[c], "dp", peer
        ).start()

    def look_back(c):
        for i in range(N_DP):
            reach = (i + 1) * ROWS
            inner[c, i] = dot(scores[i, :, 0:reach], scaled[c, 0:reach, :])

    def mix(c):
        arrived(states_in.at[c], N_CTX - 1, h_recv.at[c])
        carried = states_in[c].reshape(N_DP * STATE, WIDTH)
        skip = skips[c, 0:1, :]
        for i in range(N_DP):
            both = inner[c, i] + dot(reads_m[i], carried)
            factor = dot(factors[i], spread[0, c])
            mixed[c, i] = (both * factor + skip * xs[c, i].astype(F32)).astype(BF16)

            @pl.when((me != i) & (c < CHUNKS - 1))
            def _():
                remote(
                    mixed.at[c, i], landed.at[c, me], y_send.at[c], y_recv.at[c], "dp", i
                ).start()

            @pl.when((me != i) & (c == CHUNKS - 1))
            def _():
                remote(
                    mixed.at[c, i], last_ref.at[me], y_send.at[c], y_recv.at[c], "dp", i
                ).start()

        @pl.when(c < CHUNKS - 1)
        def _():
            landed[c, me] = mixed[c, me]

    def step(s, carry):
        @pl.when(s < CHUNKS)
        def _():
            summarize(s)

        @pl.when((s > 0) & (s < CHUNKS + 1))
        def _():
            carry_on(s - 1)

        @pl.when(s > 1)
        def _():
            mix(s - 2)

        @pl.when(s < CHUNKS)
        def _():
            look_back(s)

        return carry

    lax.fori_loop(0, CHUNKS + 2, step, 0)

    last_copy = pltpu.make_async_copy(
        mixed.at[CHUNKS - 1, me], last_ref.at[me], local_sem.at[3]
    )
    last_copy.start()
    gate_copy.wait()
    squares[...] = jnp.zeros((ROWS, 128), F32)
    results = []
    for c in range(CHUNKS - 1):
        arrived(landed.at[c], N_DP - 1, y_recv.at[c])

        def gating(g, carry):
            gate = gates[:, pl.ds(pl.multiple_of(g * 1024 + c * WIDTH, WIDTH), WIDTH)].astype(F32)
            gated = landed[c, g].astype(F32) * silu(gate)
            landed[c, g] = gated.astype(BF16)
            total = jnp.sum(gated * gated, axis=1, keepdims=True)
            squares[...] += jnp.where(iota((ROWS, 128), 1) == g, total, 0.0)
            return carry

        lax.fori_loop(0, GROUPS, gating, 0)
        results.append(pltpu.make_async_copy(landed.at[c], gated_ref.at[c], done_sem.at[c]))
        results[-1].start()
    results.append(pltpu.make_async_copy(squares, squares_ref, done_sem.at[CHUNKS - 1]))
    results[-1].start()
    for copy in results:
        copy.wait()
    last_copy.wait()
    arrived(mixed.at[CHUNKS - 1], N_DP - 1, y_recv.at[CHUNKS - 1])

    arrived(meta, N_DP - 1, send_sem.at[0])
    arrived(writes, N_DP - 1, send_sem.at[1])
    arrived(reads, N_DP - 1, send_sem.at[2])
    arrived(aux_in, N_CTX - 1, send_sem.at[3])
    for c in range(CHUNKS):
        arrived(xs.at[c], N_DP - 1, x_send.at[c])
        arrived(sums_in.at[c], N_CTX - 1, s_send.at[c])
        arrived(states_in.at[c], N_CTX - 1, h_send.at[c])
        arrived(mixed.at[c], N_DP - 1, y_send.at[c])


def finish(
    gated_hbm,
    squares_ref,
    last_hbm,
    gate_hbm,
    gain_ref,
    out_ref,
    gated,
    lasts,
    gates,
    done,
    load_sem,
    done_sem,
):
    early = WIDTH * (CHUNKS - 1)

    def loads(g):
        start = pl.multiple_of(g * 1024 + early, WIDTH)
        return [
            pltpu.make_async_copy(gate_hbm.at[:, pl.ds(start, WIDTH)], gates.at[g], load_sem.at[0, g]),
            pltpu.make_async_copy(last_hbm.at[g], lasts.at[g], load_sem.at[1, g]),
            pltpu.make_async_copy(gated_hbm.at[:, g], gated.at[g], load_sem.at[2, g]),
        ]

    def result(g):
        place = pl.ds(pl.multiple_of(g * 1024, 1024), 1024)
        return pltpu.make_async_copy(done.at[g], out_ref.at[:, place], done_sem.at[g])

    for g in range(GROUPS):
        for copy in loads(g):
            copy.start()

    def group(g, carry):
        for copy in loads(g):
            copy.wait()
        late = lasts[g].astype(F32) * silu(gates[g].astype(F32))
        total = jnp.where(iota((ROWS, 128), 1) == g, squares_ref[...], 0.0)
        for k in range(WIDTH // 128):
            total = total + late[:, k * 128 : (k + 1) * 128] * late[:, k * 128 : (k + 1) * 128]
        inverse = lax.rsqrt(jnp.sum(total, axis=1, keepdims=True) * (1.0 / 1024.0) + EPSILON)
        for c in range(CHUNKS):
            part = gated[g, c].astype(F32) if c < CHUNKS - 1 else late
            gain = gain_ref[:, pl.ds(pl.multiple_of(g * 1024 + c * WIDTH, WIDTH), WIDTH)]
            done[g, :, c * WIDTH : (c + 1) * WIDTH] = (part * inverse * gain).astype(BF16)
        result(g).start()
        return carry

    lax.fori_loop(0, GROUPS, group, 0)
    for g in range(GROUPS):
        result(g).wait()


def shards(
    ssm_input,
    gate_input,
    write_basis,
    read_basis,
    step_size,
    decay_rate,
    skip_weight,
    norm_gain,
    row_owner,
    document_lengths,
):
    hbm = pl.BlockSpec(memory_space=pltpu.HBM)
    anywhere = pl.BlockSpec(memory_space=pl.ANY)
    vmem = pl.BlockSpec(memory_space=pltpu.VMEM)
    dma = pltpu.SemaphoreType.DMA
    gated, squares, last = pl.pallas_call(
        kernel,
        out_shape=[
            jax.ShapeDtypeStruct((CHUNKS - 1, GROUPS, ROWS, WIDTH), BF16),
            jax.ShapeDtypeStruct((ROWS, 128), F32),
            jax.ShapeDtypeStruct((GROUPS, ROWS, WIDTH), BF16),
        ],
        in_specs=[hbm] * 9,
        out_specs=[anywhere] * 3,
        scratch_shapes=[
            pltpu.VMEM((ROWS, GROUPS * 1024), BF16),
            pltpu.VMEM((CHUNKS - 1, N_DP, ROWS, WIDTH), BF16),
            pltpu.VMEM((ROWS, 128), F32),
            pltpu.VMEM((1, ROWS), jnp.int32),
            pltpu.VMEM((1, DOCS), jnp.int32),
            pltpu.VMEM((1, 128), F32),
            pltpu.VMEM((1, 128), F32),
            pltpu.VMEM((ROWS, 128), BF16),
            pltpu.VMEM((N_DP, 32, ROWS), BF16),
            pltpu.VMEM((CHUNKS, 8, WIDTH), F32),
            pltpu.VMEM((N_DP, 32, ROWS), BF16),
            pltpu.VMEM((N_DP, ROWS, STATE), BF16),
            pltpu.VMEM((N_DP, ROWS, STATE), BF16),
            pltpu.VMEM((CHUNKS, N_DP, ROWS, WIDTH), BF16),
            pltpu.VMEM((N_DP, 8, 1024), F32),
            pltpu.VMEM((N_CTX, 8, 1024), F32),
            pltpu.VMEM((CHUNKS, N_CTX, 64, WIDTH), BF16),
            pltpu.VMEM((CHUNKS, N_CTX, 64, WIDTH), BF16),
            pltpu.VMEM((CHUNKS, N_CTX, 64, WIDTH), BF16),
            pltpu.VMEM((CHUNKS, N_CTX, 64, WIDTH), BF16),
            pltpu.VMEM((CHUNKS, N_DP, ROWS, WIDTH), BF16),
            pltpu.VMEM((N_DP, ROWS, N_DP * ROWS), BF16),
            pltpu.VMEM((CHUNKS, N_DP * ROWS, WIDTH), BF16),
            pltpu.VMEM((N_DP // 2, 2 * STATE, N_DP * ROWS), BF16),
            pltpu.VMEM((N_DP, ROWS, N_DP * STATE), BF16),
            pltpu.VMEM((N_DP, ROWS, 128), BF16),
            pltpu.VMEM((N_DP, ROWS), F32),
            pltpu.VMEM((N_DP, ROWS, 128), F32),
            pltpu.VMEM((2, CHUNKS, 128, WIDTH), BF16),
            pltpu.VMEM((CHUNKS, N_DP, ROWS, WIDTH), F32),
            dma((1,)),
            dma((CHUNKS,)),
            dma((4,)),
            dma((4 + CHUNKS,)),
            dma((4,)),
            dma((4,)),
            dma((CHUNKS,)),
            dma((CHUNKS,)),
            dma((CHUNKS,)),
            dma((CHUNKS,)),
            dma((CHUNKS,)),
            dma((CHUNKS,)),
            dma((CHUNKS,)),
            dma((CHUNKS,)),
        ],
        compiler_params=pltpu.CompilerParams(
            collective_id=0, has_side_effects=True, vmem_limit_bytes=60 * 2**20
        ),
        cost_estimate=pl.CostEstimate(
            flops=14 * 10**9, bytes_accessed=16 * 2**20, transcendentals=4 * 10**6
        ),
    )(
        ssm_input,
        write_basis,
        read_basis,
        step_size,
        row_owner.reshape(1, -1),
        document_lengths,
        decay_rate.reshape(1, -1),
        skip_weight.reshape(1, -1),
        gate_input,
    )
    return pl.pallas_call(
        finish,
        out_shape=jax.ShapeDtypeStruct((ROWS, GROUPS * 1024), BF16),
        in_specs=[anywhere, vmem, anywhere, anywhere, vmem],
        out_specs=anywhere,
        scratch_shapes=[
            pltpu.VMEM((GROUPS, CHUNKS - 1, ROWS, WIDTH), BF16),
            pltpu.VMEM((GROUPS, ROWS, WIDTH), BF16),
            pltpu.VMEM((GROUPS, ROWS, WIDTH), BF16),
            pltpu.VMEM((GROUPS, ROWS, 1024), BF16),
            dma((3, GROUPS)),
            dma((GROUPS,)),
        ],
        compiler_params=pltpu.CompilerParams(vmem_limit_bytes=60 * 2**20),
        cost_estimate=pl.CostEstimate(
            flops=20 * 2**20, bytes_accessed=12 * 2**20, transcendentals=2 * 2**20
        ),
    )(gated, squares, last, gate_input, norm_gain.reshape(1, -1))


def solution(mesh):
    placed = (
        P(("dp", "ctx"), None),
        P(("dp", "ctx"), None),
        P(("dp", "ctx"), None),
        P(("dp", "ctx"), None),
        P(("dp", "ctx"), None),
        P(),
        P(),
        P(),
        P(("dp", "ctx"), None),
        P("dp", None),
    )
    return jax.shard_map(
        shards, mesh=mesh, in_specs=placed, out_specs=P(("dp", "ctx"), None), check_vma=False
    )
```

```python
import jax
import jax.numpy as jnp
from jax import lax
from jax.experimental import pallas as pl
from jax.experimental.pallas import tpu as pltpu
from jax.sharding import PartitionSpec as P

GROUPS = 8
BLOCK = 512
EPSILON = 1e-05
CHUNKS = 4
N_DP = 8
N_CTX = 16
ROWS = 256
HEADS = 16
WIDTH = 1024 // CHUNKS
STATE = 128
DOCS = 8
SLOTS = 64
MESH = pl.DeviceIdType.MESH
F32 = jnp.float32
BF16 = jnp.bfloat16


def dot(a, b, dims=((1,), (0,)), precision=None):
    return lax.dot_general(a, b, (dims, ((), ())), precision=precision, preferred_element_type=F32)


def exact(a, b, dims=((1,), (0,))):
    return dot(a, b, dims, lax.Precision.HIGHEST)


def thirds(value):
    high = value.astype(BF16).astype(F32)
    middle = (value - high).astype(BF16).astype(F32)
    low = (value - high - middle).astype(BF16).astype(F32)
    return high, middle, low


def silu(value):
    return value / (1.0 + jnp.exp(-value))


def iota(shape, dim):
    return lax.broadcasted_iota(jnp.int32, shape, dim)


def kernel(
    x_ref,
    write_ref,
    read_ref,
    step_ref,
    owner_hbm,
    length_hbm,
    rate_hbm,
    skip_hbm,
    gate_hbm,
    gated_ref,
    squares_ref,
    last_ref,
    gates,
    landed,
    squares,
    owner_ref,
    length_ref,
    rate_ref,
    skip_ref,
    steps,
    packet,
    skips,
    meta,
    writes,
    reads,
    xs,
    aux,
    aux_in,
    sums,
    sums_in,
    states,
    states_in,
    mixed,
    scores,
    scaled,
    writes_t,
    reads_m,
    factors,
    keys_row,
    keys_col,
    spread,
    inner,
    gate_sem,
    done_sem,
    small_sem,
    local_sem,
    send_sem,
    recv_sem,
    x_send,
    x_recv,
    s_send,
    s_recv,
    h_send,
    h_recv,
    y_send,
    y_recv,
):
    me = lax.axis_index("dp")
    col = lax.axis_index("ctx")

    def remote(src, dst, send, recv, axis, peer):
        return pltpu.make_async_remote_copy(
            src_ref=src,
            dst_ref=dst,
            send_sem=send,
            recv_sem=recv,
            device_id={axis: peer},
            device_id_type=MESH,
        )

    def lanes(ref, start, width):
        return ref.at[:, pl.ds(pl.multiple_of(start, 128), width)]

    def piece(ref, owner, c):
        return lanes(ref, owner * 1024 + c * WIDTH, WIDTH)

    barrier = pltpu.get_barrier_semaphore()
    for d in range(1, N_DP):
        pl.semaphore_signal(
            barrier, inc=1, device_id={"dp": lax.rem(me + d, N_DP)}, device_id_type=MESH
        )
    for d in range(1, N_CTX):
        pl.semaphore_signal(
            barrier, inc=1, device_id={"ctx": lax.rem(col + d, N_CTX)}, device_id_type=MESH
        )

    own = [
        pltpu.make_async_copy(step_ref, steps, local_sem.at[0]),
        pltpu.make_async_copy(lanes(write_ref, me * STATE, STATE), writes.at[me], local_sem.at[1]),
        pltpu.make_async_copy(lanes(read_ref, me * STATE, STATE), reads.at[me], local_sem.at[2]),
    ]
    own_x = [
        pltpu.make_async_copy(piece(x_ref, me, c), xs.at[c, me], local_sem.at[4 + c])
        for c in range(CHUNKS)
    ]
    small = [
        pltpu.make_async_copy(owner_hbm, owner_ref, small_sem.at[0]),
        pltpu.make_async_copy(length_hbm, length_ref, small_sem.at[1]),
        pltpu.make_async_copy(rate_hbm, rate_ref, small_sem.at[2]),
        pltpu.make_async_copy(skip_hbm, skip_ref, small_sem.at[3]),
    ]
    gate_copy = pltpu.make_async_copy(gate_hbm, gates, gate_sem.at[0])
    for copy in own[:1] + small + own[1:] + own_x + [gate_copy]:
        copy.start()
    pl.semaphore_wait(barrier, N_DP + N_CTX - 2)

    for d in range(1, N_DP):
        peer = lax.rem(me + d, N_DP)
        remote(
            lanes(write_ref, peer * STATE, STATE),
            writes.at[me],
            send_sem.at[1],
            recv_sem.at[1],
            "dp",
            peer,
        ).start()
        remote(
            lanes(read_ref, peer * STATE, STATE),
            reads.at[me],
            send_sem.at[2],
            recv_sem.at[2],
            "dp",
            peer,
        ).start()

    own[0].wait()
    for copy in small:
        copy.wait()
    packet[:, :, 0:ROWS] = steps[...].astype(F32).T.reshape(GROUPS, HEADS, ROWS).astype(BF16)
    owner_row = owner_ref[...].astype(F32)
    line = iota((HEADS, 128), 0)
    lane = iota((HEADS, 128), 1)
    extra = jnp.where(line == 0, owner_row[:, 0:128], 0.0)
    extra = jnp.where(line == 1, owner_row[:, 128:256], extra)
    for d in range(DOCS):
        length = length_ref[0:1, d : d + 1]
        extra = jnp.where((line == 2) & (lane == d), (length // 64).astype(F32), extra)
        extra = jnp.where((line == 3) & (lane == d), (length % 64).astype(F32), extra)
    for k in range(GROUPS):
        packet[k, :, ROWS : ROWS + 128] = extra.astype(BF16)
    for d in range(1, N_DP):
        peer = lax.rem(me + d, N_DP)
        remote(
            packet.at[peer], meta.at[me], send_sem.at[0], recv_sem.at[0], "dp", peer
        ).start()
    meta[me] = packet[me]
    for c in range(CHUNKS):
        for d in range(1, N_DP):
            peer = lax.rem(me + d, N_DP)
            remote(
                piece(x_ref, peer, c), xs.at[c, me], x_send.at[c], x_recv.at[c], "dp", peer
            ).start()

    row = iota((128, WIDTH), 0)
    for c in range(CHUNKS):
        head = c * (HEADS // CHUNKS) + iota((128, WIDTH), 1) // 64
        named = lax.rem(row, HEADS) == head
        spread[0, c] = jnp.where(named & (row < 48), 1.0, 0.0).astype(BF16)
        spread[1, c] = jnp.where(named & (row >= 48) & (row < 96), 1.0, 0.0).astype(BF16)
        mine = jnp.where(row == me * HEADS + head, 1.0, 0.0)
        skips[c] = exact(jnp.broadcast_to(skip_ref[...], (8, 128)), mine)

    def arrived(ref, count, sem):
        part = ref.at[pl.ds(0, count)]
        pltpu.make_async_copy(part, part, sem).wait()

    arrived(meta, N_DP - 1, recv_sem.at[0])
    first_slot = (col * BLOCK).astype(F32)

    extras = meta[:, :, ROWS : ROWS + 128].astype(F32)
    owners = jnp.concatenate([extras[:, 0, :], extras[:, 1, :]], axis=1)
    lengths = extras[:, 2, :] * 64.0 + extras[:, 3, :]
    starts = []
    total = jnp.zeros((N_DP, 1), F32)
    for d in range(DOCS):
        starts.append(total)
        total = total + lengths[:, d : d + 1]
    sequence = iota((N_DP, 1), 0).astype(F32)
    table = jnp.where(
        owners[:, None, :] == iota((N_DP, N_DP, ROWS), 1).astype(F32), 1.0, 0.0
    )
    earlier = jnp.where(iota((ROWS, ROWS), 0) < iota((ROWS, ROWS), 1), 1.0, 0.0)
    counts = dot(table.reshape(N_DP * N_DP, ROWS).astype(BF16), earlier.astype(BF16))
    rank = jnp.sum(table * counts.reshape(N_DP, N_DP, ROWS), axis=1)
    slot = first_slot + (iota((N_DP, ROWS), 0) * SLOTS).astype(F32) + rank
    segment = jnp.zeros((N_DP, N_DP, ROWS), F32)
    before = jnp.zeros((N_DP, 1), F32)
    end = jnp.zeros((N_DP, 1), F32)
    for d in range(DOCS):
        segment = segment + jnp.where(slot[:, None, :] >= starts[d][None], 1.0, 0.0)
        before = before + jnp.where(first_slot - 1.0 >= starts[d], 1.0, 0.0)
        end = end + jnp.where(first_slot + (BLOCK - 1.0) >= starts[d], 1.0, 0.0)
    key = owners * 16.0 + jnp.sum(table * segment, axis=1)
    key_before = sequence * 16.0 + before
    key_end = sequence * 16.0 + end
    same_document = jnp.where(key_before == key_end, 1.0, 0.0)
    keys_row[...] = key
    key_t = key.T
    owner_t = owners.T

    rate = jnp.sum(
        jnp.where(
            iota((HEADS, 128), 1) == iota((HEADS, 128), 0) + me * HEADS, rate_ref[...], 0.0
        ),
        axis=1,
        keepdims=True,
    )
    rate_row = jnp.sum(
        jnp.where(iota((HEADS, HEADS), 0) == iota((HEADS, HEADS), 1), rate, 0.0),
        axis=0,
        keepdims=True,
    )
    not_later = iota((ROWS, ROWS), 0) <= iota((ROWS, ROWS), 1)
    sofar = jnp.zeros((HEADS, N_DP), F32)
    whole_t = jnp.zeros((N_DP, HEADS), F32)
    running = []
    for i in range(N_DP):
        keys_col[i] = jnp.broadcast_to(key_t[:, i : i + 1], (ROWS, 128))
        step = meta[i, :, 0:ROWS]
        owned = table[i]
        same = jnp.where((owner_t[:, i : i + 1] == owners[i : i + 1, :]) & not_later, 1.0, 0.0)
        running.append(dot(step, same.astype(BF16)) + exact(sofar, owned))
        sofar = sofar + dot(step, owned.astype(BF16), ((1,), (1,)))
        whole_t = whole_t + dot(owned.astype(BF16), step, ((1,), (1,)))
    middle = -0.5 * rate * sofar
    for i in range(N_DP):
        exponent = -rate * running[i] - exact(middle, table[i])
        rising = thirds(jnp.exp(-exponent) * meta[i, :, 0:ROWS].astype(F32))
        falling = thirds(jnp.exp(exponent))
        stack = jnp.concatenate(falling + rising + (jnp.zeros((32, ROWS), F32),), axis=0)
        factors[i] = stack.T.astype(BF16)
    middle_t = -0.5 * whole_t * rate_row
    half_decay = thirds(jnp.exp(middle_t))
    full_decay = thirds(jnp.exp(2.0 * middle_t) * same_document)
    for c in range(CHUNKS):
        heads = spread[0, c, 0:HEADS, :]
        half = sum(dot(part.astype(BF16), heads) for part in half_decay)
        full = sum(dot(part.astype(BF16), heads) for part in full_decay)
        for k in range(N_DP):
            aux[k, 0:1, c * WIDTH : (c + 1) * WIDTH] = full[k : k + 1, :]
            aux[k, 1:2, c * WIDTH : (c + 1) * WIDTH] = half[k : k + 1, :]
    for k in range(N_DP):
        aux[k, 2:8, :] = jnp.zeros((6, 1024), F32)
    for d in range(1, N_CTX):
        peer = lax.rem(col + d, N_CTX)
        remote(
            aux.at[peer // 2], aux_in.at[col], send_sem.at[3], recv_sem.at[3], "ctx", peer
        ).start()
    aux_in[col] = aux[col // 2]

    own[1].wait()
    arrived(writes, N_DP - 1, recv_sem.at[1])
    for i in range(N_DP):
        flipped = writes[i].astype(F32).T
        for k in range(N_DP):
            kept = keys_row[i : i + 1, :] == key_end[k : k + 1, :]
            half = pl.ds((k % 2) * STATE, STATE)
            writes_t[k // 2, half, i * ROWS : (i + 1) * ROWS] = jnp.where(
                kept, flipped, 0.0
            ).astype(BF16)
    own[2].wait()
    arrived(reads, N_DP - 1, recv_sem.at[2])

    for i in range(N_DP):
        block = reads[i].astype(F32)
        for k in range(N_DP):
            kept = keys_col[i] == key_before[k : k + 1, :]
            reads_m[i, :, k * STATE : (k + 1) * STATE] = jnp.where(kept, block, 0.0).astype(BF16)

    ordered = iota((ROWS, ROWS), 0) >= iota((ROWS, ROWS), 1)

    def score_rows(i, carry):
        key_q = keys_col[i][:, 0:1]
        block = reads[i]

        def score(j, carry):
            raw = dot(block, writes[j], ((1,), (1,)))
            kept = (key_q == keys_row[pl.ds(j, 1), :]) & (ordered | (j < i))
            scores[i, :, pl.ds(pl.multiple_of(j * ROWS, ROWS), ROWS)] = jnp.where(
                kept, raw, 0.0
            ).astype(BF16)
            return carry

        return lax.fori_loop(0, i + 1, score, carry)

    lax.fori_loop(0, N_DP, score_rows, 0)

    def summarize(c):
        pltpu.make_async_copy(xs.at[0, 0], xs.at[0, 0], local_sem.at[4 + c]).wait()
        arrived(xs.at[c], N_DP - 1, x_recv.at[c])

        def scale(i, carry):
            factor = dot(factors[i], spread[1, c])
            scaled[c, pl.ds(pl.multiple_of(i * ROWS, ROWS), ROWS), :] = (
                xs[c, i].astype(F32) * factor
            ).astype(BF16)
            return carry

        lax.fori_loop(0, N_DP, scale, 0)

        def collect(k, carry):
            pair = lax.rem(k + col // 4, N_DP // 2)
            part = dot(writes_t[pair], scaled[c])
            for side in range(4):
                peer = 4 * pair + side
                half = aux[
                    2 * pair + side // 2, 1:2, pl.ds(pl.multiple_of(c * WIDTH, WIDTH), WIDTH)
                ]
                sums[c, peer] = (part[64 * side : 64 * side + 64] * half).astype(BF16)

                @pl.when(peer != col)
                def _():
                    remote(
                        sums.at[c, peer], sums_in.at[c, col], s_send.at[c], s_recv.at[c], "ctx", peer
                    ).start()

            return carry

        lax.fori_loop(0, N_DP // 2, collect, 0)
        sums_in[c, col] = sums[c, col]

    def carry_on(c):
        @pl.when(c == 0)
        def _():
            arrived(aux_in, N_CTX - 1, recv_sem.at[3])

        arrived(sums_in.at[c], N_CTX - 1, s_recv.at[c])
        window = pl.ds(pl.multiple_of(c * WIDTH, WIDTH), WIDTH)

        def advance(j, held):
            states[c, j] = (held * aux_in[j, 1:2, window]).astype(BF16)
            return held * aux_in[j, 0:1, window] + sums_in[c, j].astype(F32)

        lax.fori_loop(0, N_CTX, advance, jnp.zeros((64, WIDTH), F32))
        for d in range(1, N_CTX):
            peer = lax.rem(col + d, N_CTX)
            remote(
                states.at[c, peer], states_in.at[c, col], h_send.at[c], h_recv.at[c], "ctx", peer
            ).start()
        states_in[c, col] = states[c, col]

    def hand_back(c, peer):
        remote(
            mixed.at[c, peer], piece(out_ref, me, c), y_send.at[c], y_recv.at[c], "dp", peer
        ).start()

    def look_back(c):
        for i in range(N_DP):
            reach = (i + 1) * ROWS
            inner[c, i] = dot(scores[i, :, 0:reach], scaled[c, 0:reach, :])

    def mix(c):
        arrived(states_in.at[c], N_CTX - 1, h_recv.at[c])
        carried = states_in[c].reshape(N_DP * STATE, WIDTH)
        skip = skips[c, 0:1, :]
        for i in range(N_DP):
            both = inner[c, i] + dot(reads_m[i], carried)
            factor = dot(factors[i], spread[0, c])
            mixed[c, i] = (both * factor + skip * xs[c, i].astype(F32)).astype(BF16)

            @pl.when((me != i) & (c < CHUNKS - 1))
            def _():
                remote(
                    mixed.at[c, i], landed.at[c, me], y_send.at[c], y_recv.at[c], "dp", i
                ).start()

            @pl.when((me != i) & (c == CHUNKS - 1))
            def _():
                remote(
                    mixed.at[c, i], last_ref.at[me], y_send.at[c], y_recv.at[c], "dp", i
                ).start()

        @pl.when(c < CHUNKS - 1)
        def _():
            landed[c, me] = mixed[c, me]

    def step(s, carry):
        @pl.when(s < CHUNKS)
        def _():
            summarize(s)

        @pl.when((s > 0) & (s < CHUNKS + 1))
        def _():
            carry_on(s - 1)

        @pl.when(s > 1)
        def _():
            mix(s - 2)

        @pl.when(s < CHUNKS)
        def _():
            look_back(s)

        return carry

    lax.fori_loop(0, CHUNKS + 2, step, 0)

    last_copy = pltpu.make_async_copy(
        mixed.at[CHUNKS - 1, me], last_ref.at[me], local_sem.at[3]
    )
    last_copy.start()
    gate_copy.wait()
    squares[...] = jnp.zeros((ROWS, 128), F32)
    results = []
    for c in range(CHUNKS - 1):
        arrived(landed.at[c], N_DP - 1, y_recv.at[c])

        def gating(g, carry):
            gate = gates[:, pl.ds(pl.multiple_of(g * 1024 + c * WIDTH, WIDTH), WIDTH)].astype(F32)
            gated = landed[c, g].astype(F32) * silu(gate)
            landed[c, g] = gated.astype(BF16)
            total = jnp.sum(gated * gated, axis=1, keepdims=True)
            squares[...] += jnp.where(iota((ROWS, 128), 1) == g, total, 0.0)
            return carry

        lax.fori_loop(0, GROUPS, gating, 0)
        results.append(pltpu.make_async_copy(landed.at[c], gated_ref.at[c], done_sem.at[c]))
        results[-1].start()
    results.append(pltpu.make_async_copy(squares, squares_ref, done_sem.at[CHUNKS - 1]))
    results[-1].start()
    for copy in results:
        copy.wait()
    last_copy.wait()
    arrived(mixed.at[CHUNKS - 1], N_DP - 1, y_recv.at[CHUNKS - 1])

    arrived(meta, N_DP - 1, send_sem.at[0])
    arrived(writes, N_DP - 1, send_sem.at[1])
    arrived(reads, N_DP - 1, send_sem.at[2])
    arrived(aux_in, N_CTX - 1, send_sem.at[3])
    for c in range(CHUNKS):
        arrived(xs.at[c], N_DP - 1, x_send.at[c])
        arrived(sums_in.at[c], N_CTX - 1, s_send.at[c])
        arrived(states_in.at[c], N_CTX - 1, h_send.at[c])
        arrived(mixed.at[c], N_DP - 1, y_send.at[c])


def finish(
    gated_hbm,
    squares_ref,
    last_hbm,
    gate_hbm,
    gain_ref,
    out_ref,
    gated,
    lasts,
    gates,
    done,
    load_sem,
    done_sem,
):
    early = WIDTH * (CHUNKS - 1)

    def loads(g):
        start = pl.multiple_of(g * 1024 + early, WIDTH)
        return [
            pltpu.make_async_copy(gate_hbm.at[:, pl.ds(start, WIDTH)], gates.at[g], load_sem.at[0, g]),
            pltpu.make_async_copy(last_hbm.at[g], lasts.at[g], load_sem.at[1, g]),
            pltpu.make_async_copy(gated_hbm.at[:, g], gated.at[g], load_sem.at[2, g]),
        ]

    def result(g):
        place = pl.ds(pl.multiple_of(g * 1024, 1024), 1024)
        return pltpu.make_async_copy(done.at[g], out_ref.at[:, place], done_sem.at[g])

    for g in range(GROUPS):
        for copy in loads(g):
            copy.start()

    def group(g, carry):
        for copy in loads(g):
            copy.wait()
        late = lasts[g].astype(F32) * silu(gates[g].astype(F32))
        total = jnp.where(iota((ROWS, 128), 1) == g, squares_ref[...], 0.0)
        for k in range(WIDTH // 128):
            total = total + late[:, k * 128 : (k + 1) * 128] * late[:, k * 128 : (k + 1) * 128]
        inverse = lax.rsqrt(jnp.sum(total, axis=1, keepdims=True) * (1.0 / 1024.0) + EPSILON)
        for c in range(CHUNKS):
            part = gated[g, c].astype(F32) if c < CHUNKS - 1 else late
            gain = gain_ref[:, pl.ds(pl.multiple_of(g * 1024 + c * WIDTH, WIDTH), WIDTH)]
            done[g, :, c * WIDTH : (c + 1) * WIDTH] = (part * inverse * gain).astype(BF16)
        result(g).start()
        return carry

    lax.fori_loop(0, GROUPS, group, 0)
    for g in range(GROUPS):
        result(g).wait()


def shards(
    ssm_input,
    gate_input,
    write_basis,
    read_basis,
    step_size,
    decay_rate,
    skip_weight,
    norm_gain,
    row_owner,
    document_lengths,
):
    hbm = pl.BlockSpec(memory_space=pltpu.HBM)
    anywhere = pl.BlockSpec(memory_space=pl.ANY)
    vmem = pl.BlockSpec(memory_space=pltpu.VMEM)
    dma = pltpu.SemaphoreType.DMA
    gated, squares, last = pl.pallas_call(
        kernel,
        out_shape=[
            jax.ShapeDtypeStruct((CHUNKS - 1, GROUPS, ROWS, WIDTH), BF16),
            jax.ShapeDtypeStruct((ROWS, 128), F32),
            jax.ShapeDtypeStruct((GROUPS, ROWS, WIDTH), BF16),
        ],
        in_specs=[hbm] * 9,
        out_specs=[anywhere] * 3,
        scratch_shapes=[
            pltpu.VMEM((ROWS, GROUPS * 1024), BF16),
            pltpu.VMEM((CHUNKS - 1, N_DP, ROWS, WIDTH), BF16),
            pltpu.VMEM((ROWS, 128), F32),
            pltpu.VMEM((1, ROWS), jnp.int32),
            pltpu.VMEM((1, DOCS), jnp.int32),
            pltpu.VMEM((1, 128), F32),
            pltpu.VMEM((1, 128), F32),
            pltpu.VMEM((ROWS, 128), BF16),
            pltpu.VMEM((N_DP, HEADS, ROWS + 128), BF16),
            pltpu.VMEM((CHUNKS, 8, WIDTH), F32),
            pltpu.VMEM((N_DP, HEADS, ROWS + 128), BF16),
            pltpu.VMEM((N_DP, ROWS, STATE), BF16),
            pltpu.VMEM((N_DP, ROWS, STATE), BF16),
            pltpu.VMEM((CHUNKS, N_DP, ROWS, WIDTH), BF16),
            pltpu.VMEM((N_DP, 8, 1024), F32),
            pltpu.VMEM((N_CTX, 8, 1024), F32),
            pltpu.VMEM((CHUNKS, N_CTX, 64, WIDTH), BF16),
            pltpu.VMEM((CHUNKS, N_CTX, 64, WIDTH), BF16),
            pltpu.VMEM((CHUNKS, N_CTX, 64, WIDTH), BF16),
            pltpu.VMEM((CHUNKS, N_CTX, 64, WIDTH), BF16),
            pltpu.VMEM((CHUNKS, N_DP, ROWS, WIDTH), BF16),
            pltpu.VMEM((N_DP, ROWS, N_DP * ROWS), BF16),
            pltpu.VMEM((CHUNKS, N_DP * ROWS, WIDTH), BF16),
            pltpu.VMEM((N_DP // 2, 2 * STATE, N_DP * ROWS), BF16),
            pltpu.VMEM((N_DP, ROWS, N_DP * STATE), BF16),
            pltpu.VMEM((N_DP, ROWS, 128), BF16),
            pltpu.VMEM((N_DP, ROWS), F32),
            pltpu.VMEM((N_DP, ROWS, 128), F32),
            pltpu.VMEM((2, CHUNKS, 128, WIDTH), BF16),
            pltpu.VMEM((CHUNKS, N_DP, ROWS, WIDTH), F32),
            dma((1,)),
            dma((CHUNKS,)),
            dma((4,)),
            dma((4 + CHUNKS,)),
            dma((4,)),
            dma((4,)),
            dma((CHUNKS,)),
            dma((CHUNKS,)),
            dma((CHUNKS,)),
            dma((CHUNKS,)),
            dma((CHUNKS,)),
            dma((CHUNKS,)),
            dma((CHUNKS,)),
            dma((CHUNKS,)),
        ],
        compiler_params=pltpu.CompilerParams(
            collective_id=0, has_side_effects=True, vmem_limit_bytes=60 * 2**20
        ),
        cost_estimate=pl.CostEstimate(
            flops=14 * 10**9, bytes_accessed=16 * 2**20, transcendentals=4 * 10**6
        ),
    )(
        ssm_input,
        write_basis,
        read_basis,
        step_size,
        row_owner.reshape(1, -1),
        document_lengths,
        decay_rate.reshape(1, -1),
        skip_weight.reshape(1, -1),
        gate_input,
    )
    return pl.pallas_call(
        finish,
        out_shape=jax.ShapeDtypeStruct((ROWS, GROUPS * 1024), BF16),
        in_specs=[anywhere, vmem, anywhere, anywhere, vmem],
        out_specs=anywhere,
        scratch_shapes=[
            pltpu.VMEM((GROUPS, CHUNKS - 1, ROWS, WIDTH), BF16),
            pltpu.VMEM((GROUPS, ROWS, WIDTH), BF16),
            pltpu.VMEM((GROUPS, ROWS, WIDTH), BF16),
            pltpu.VMEM((GROUPS, ROWS, 1024), BF16),
            dma((3, GROUPS)),
            dma((GROUPS,)),
        ],
        compiler_params=pltpu.CompilerParams(vmem_limit_bytes=60 * 2**20),
        cost_estimate=pl.CostEstimate(
            flops=20 * 2**20, bytes_accessed=12 * 2**20, transcendentals=2 * 2**20
        ),
    )(gated, squares, last, gate_input, norm_gain.reshape(1, -1))


def solution(mesh):
    placed = (
        P(("dp", "ctx"), None),
        P(("dp", "ctx"), None),
        P(("dp", "ctx"), None),
        P(("dp", "ctx"), None),
        P(("dp", "ctx"), None),
        P(),
        P(),
        P(),
        P(("dp", "ctx"), None),
        P("dp", None),
    )
    return jax.shard_map(
        shards, mesh=mesh, in_specs=placed, out_specs=P(("dp", "ctx"), None), check_vma=False
    )
```

```python
import jax
import jax.numpy as jnp
from jax import lax
from jax.experimental import pallas as pl
from jax.experimental.pallas import tpu as pltpu
from jax.sharding import PartitionSpec as P

GROUPS = 8
BLOCK = 512
EPSILON = 1e-05
CHUNKS = 4
N_DP = 8
N_CTX = 16
ROWS = 256
HEADS = 16
WIDTH = 1024 // CHUNKS
STATE = 128
DOCS = 8
SLOTS = 64
MESH = pl.DeviceIdType.MESH
F32 = jnp.float32
BF16 = jnp.bfloat16


def dot(a, b, dims=((1,), (0,)), precision=None):
    return lax.dot_general(a, b, (dims, ((), ())), precision=precision, preferred_element_type=F32)


def exact(a, b, dims=((1,), (0,))):
    return dot(a, b, dims, lax.Precision.HIGHEST)


def thirds(value):
    high = value.astype(BF16).astype(F32)
    middle = (value - high).astype(BF16).astype(F32)
    low = (value - high - middle).astype(BF16).astype(F32)
    return high, middle, low


def silu(value):
    return value / (1.0 + jnp.exp(-value))


def iota(shape, dim):
    return lax.broadcasted_iota(jnp.int32, shape, dim)


def kernel(
    x_ref,
    write_ref,
    read_ref,
    step_ref,
    owner_hbm,
    length_hbm,
    rate_hbm,
    skip_hbm,
    gate_hbm,
    gated_ref,
    squares_ref,
    last_ref,
    gates,
    landed,
    squares,
    owner_ref,
    length_ref,
    rate_ref,
    skip_ref,
    steps,
    packet,
    skips,
    meta,
    writes,
    reads,
    xs,
    aux,
    aux_in,
    sums,
    sums_in,
    states,
    states_in,
    mixed,
    scores,
    scaled,
    writes_t,
    reads_m,
    factors,
    keys_row,
    keys_col,
    spread,
    inner,
    gate_sem,
    done_sem,
    small_sem,
    local_sem,
    send_sem,
    recv_sem,
    x_send,
    x_recv,
    s_send,
    s_recv,
    h_send,
    h_recv,
    y_send,
    y_recv,
):
    me = lax.axis_index("dp")
    col = lax.axis_index("ctx")

    def remote(src, dst, send, recv, axis, peer):
        return pltpu.make_async_remote_copy(
            src_ref=src,
            dst_ref=dst,
            send_sem=send,
            recv_sem=recv,
            device_id={axis: peer},
            device_id_type=MESH,
        )

    def lanes(ref, start, width):
        return ref.at[:, pl.ds(pl.multiple_of(start, 128), width)]

    def piece(ref, owner, c):
        return lanes(ref, owner * 1024 + c * WIDTH, WIDTH)

    barrier = pltpu.get_barrier_semaphore()
    for d in range(1, N_DP):
        pl.semaphore_signal(
            barrier, inc=1, device_id={"dp": lax.rem(me + d, N_DP)}, device_id_type=MESH
        )
    for d in range(1, N_CTX):
        pl.semaphore_signal(
            barrier, inc=1, device_id={"ctx": lax.rem(col + d, N_CTX)}, device_id_type=MESH
        )

    own = [
        pltpu.make_async_copy(step_ref, steps, local_sem.at[0]),
        pltpu.make_async_copy(lanes(write_ref, me * STATE, STATE), writes.at[me], local_sem.at[1]),
        pltpu.make_async_copy(lanes(read_ref, me * STATE, STATE), reads.at[me], local_sem.at[2]),
    ]
    own_x = [
        pltpu.make_async_copy(piece(x_ref, me, c), xs.at[c, me], local_sem.at[4 + c])
        for c in range(CHUNKS)
    ]
    small = [
        pltpu.make_async_copy(owner_hbm, owner_ref, small_sem.at[0]),
        pltpu.make_async_copy(length_hbm, length_ref, small_sem.at[1]),
        pltpu.make_async_copy(rate_hbm, rate_ref, small_sem.at[2]),
        pltpu.make_async_copy(skip_hbm, skip_ref, small_sem.at[3]),
    ]
    gate_copy = pltpu.make_async_copy(gate_hbm, gates, gate_sem.at[0])
    for copy in own[:1] + small:
        copy.start()
    pl.semaphore_wait(barrier, N_DP + N_CTX - 2)

    for d in range(1, N_DP):
        peer = lax.rem(me + d, N_DP)
        remote(
            lanes(write_ref, peer * STATE, STATE),
            writes.at[me],
            send_sem.at[1],
            recv_sem.at[1],
            "dp",
            peer,
        ).start()
        remote(
            lanes(read_ref, peer * STATE, STATE),
            reads.at[me],
            send_sem.at[2],
            recv_sem.at[2],
            "dp",
            peer,
        ).start()

    own[0].wait()
    for copy in small:
        copy.wait()
    packet[:, :, 0:ROWS] = steps[...].astype(F32).T.reshape(GROUPS, HEADS, ROWS).astype(BF16)
    owner_row = owner_ref[...].astype(F32)
    line = iota((HEADS, 128), 0)
    lane = iota((HEADS, 128), 1)
    extra = jnp.where(line == 0, owner_row[:, 0:128], 0.0)
    extra = jnp.where(line == 1, owner_row[:, 128:256], extra)
    for d in range(DOCS):
        length = length_ref[0:1, d : d + 1]
        extra = jnp.where((line == 2) & (lane == d), (length // 64).astype(F32), extra)
        extra = jnp.where((line == 3) & (lane == d), (length % 64).astype(F32), extra)
    for k in range(GROUPS):
        packet[k, :, ROWS : ROWS + 128] = extra.astype(BF16)
    for d in range(1, N_DP):
        peer = lax.rem(me + d, N_DP)
        remote(
            packet.at[peer], meta.at[me], send_sem.at[0], recv_sem.at[0], "dp", peer
        ).start()
    meta[me] = packet[me]
    for c in range(CHUNKS):
        for d in range(1, N_DP):
            peer = lax.rem(me + d, N_DP)
            remote(
                piece(x_ref, peer, c), xs.at[c, me], x_send.at[c], x_recv.at[c], "dp", peer
            ).start()

    for copy in own[1:] + own_x + [gate_copy]:
        copy.start()

    row = iota((128, WIDTH), 0)
    for c in range(CHUNKS):
        head = c * (HEADS // CHUNKS) + iota((128, WIDTH), 1) // 64
        named = lax.rem(row, HEADS) == head
        spread[0, c] = jnp.where(named & (row < 48), 1.0, 0.0).astype(BF16)
        spread[1, c] = jnp.where(named & (row >= 48) & (row < 96), 1.0, 0.0).astype(BF16)
        mine = jnp.where(row == me * HEADS + head, 1.0, 0.0)
        skips[c] = exact(jnp.broadcast_to(skip_ref[...], (8, 128)), mine)

    def arrived(ref, count, sem):
        part = ref.at[pl.ds(0, count)]
        pltpu.make_async_copy(part, part, sem).wait()

    arrived(meta, N_DP - 1, recv_sem.at[0])
    first_slot = (col * BLOCK).astype(F32)

    extras = meta[:, :, ROWS : ROWS + 128].astype(F32)
    owners = jnp.concatenate([extras[:, 0, :], extras[:, 1, :]], axis=1)
    lengths = extras[:, 2, :] * 64.0 + extras[:, 3, :]
    starts = []
    total = jnp.zeros((N_DP, 1), F32)
    for d in range(DOCS):
        starts.append(total)
        total = total + lengths[:, d : d + 1]
    sequence = iota((N_DP, 1), 0).astype(F32)
    table = jnp.where(
        owners[:, None, :] == iota((N_DP, N_DP, ROWS), 1).astype(F32), 1.0, 0.0
    )
    earlier = jnp.where(iota((ROWS, ROWS), 0) < iota((ROWS, ROWS), 1), 1.0, 0.0)
    counts = dot(table.reshape(N_DP * N_DP, ROWS).astype(BF16), earlier.astype(BF16))
    rank = jnp.sum(table * counts.reshape(N_DP, N_DP, ROWS), axis=1)
    slot = first_slot + (iota((N_DP, ROWS), 0) * SLOTS).astype(F32) + rank
    segment = jnp.zeros((N_DP, N_DP, ROWS), F32)
    before = jnp.zeros((N_DP, 1), F32)
    end = jnp.zeros((N_DP, 1), F32)
    for d in range(DOCS):
        segment = segment + jnp.where(slot[:, None, :] >= starts[d][None], 1.0, 0.0)
        before = before + jnp.where(first_slot - 1.0 >= starts[d], 1.0, 0.0)
        end = end + jnp.where(first_slot + (BLOCK - 1.0) >= starts[d], 1.0, 0.0)
    key = owners * 16.0 + jnp.sum(table * segment, axis=1)
    key_before = sequence * 16.0 + before
    key_end = sequence * 16.0 + end
    same_document = jnp.where(key_before == key_end, 1.0, 0.0)
    keys_row[...] = key
    key_t = key.T
    owner_t = owners.T

    rate = jnp.sum(
        jnp.where(
            iota((HEADS, 128), 1) == iota((HEADS, 128), 0) + me * HEADS, rate_ref[...], 0.0
        ),
        axis=1,
        keepdims=True,
    )
    rate_row = jnp.sum(
        jnp.where(iota((HEADS, HEADS), 0) == iota((HEADS, HEADS), 1), rate, 0.0),
        axis=0,
        keepdims=True,
    )
    not_later = iota((ROWS, ROWS), 0) <= iota((ROWS, ROWS), 1)
    sofar = jnp.zeros((HEADS, N_DP), F32)
    whole_t = jnp.zeros((N_DP, HEADS), F32)
    running = []
    for i in range(N_DP):
        keys_col[i] = jnp.broadcast_to(key_t[:, i : i + 1], (ROWS, 128))
        step = meta[i, :, 0:ROWS]
        owned = table[i]
        same = jnp.where((owner_t[:, i : i + 1] == owners[i : i + 1, :]) & not_later, 1.0, 0.0)
        running.append(dot(step, same.astype(BF16)) + exact(sofar, owned))
        sofar = sofar + dot(step, owned.astype(BF16), ((1,), (1,)))
        whole_t = whole_t + dot(owned.astype(BF16), step, ((1,), (1,)))
    middle = -0.5 * rate * sofar
    for i in range(N_DP):
        exponent = -rate * running[i] - exact(middle, table[i])
        rising = thirds(jnp.exp(-exponent) * meta[i, :, 0:ROWS].astype(F32))
        falling = thirds(jnp.exp(exponent))
        stack = jnp.concatenate(falling + rising + (jnp.zeros((32, ROWS), F32),), axis=0)
        factors[i] = stack.T.astype(BF16)
    middle_t = -0.5 * whole_t * rate_row
    half_decay = thirds(jnp.exp(middle_t))
    full_decay = thirds(jnp.exp(2.0 * middle_t) * same_document)
    for c in range(CHUNKS):
        heads = spread[0, c, 0:HEADS, :]
        half = sum(dot(part.astype(BF16), heads) for part in half_decay)
        full = sum(dot(part.astype(BF16), heads) for part in full_decay)
        for k in range(N_DP):
            aux[k, 0:1, c * WIDTH : (c + 1) * WIDTH] = full[k : k + 1, :]
            aux[k, 1:2, c * WIDTH : (c + 1) * WIDTH] = half[k : k + 1, :]
    for k in range(N_DP):
        aux[k, 2:8, :] = jnp.zeros((6, 1024), F32)
    for d in range(1, N_CTX):
        peer = lax.rem(col + d, N_CTX)
        remote(
            aux.at[peer // 2], aux_in.at[col], send_sem.at[3], recv_sem.at[3], "ctx", peer
        ).start()
    aux_in[col] = aux[col // 2]

    own[1].wait()
    arrived(writes, N_DP - 1, recv_sem.at[1])
    for i in range(N_DP):
        flipped = writes[i].astype(F32).T
        for k in range(N_DP):
            kept = keys_row[i : i + 1, :] == key_end[k : k + 1, :]
            half = pl.ds((k % 2) * STATE, STATE)
            writes_t[k // 2, half, i * ROWS : (i + 1) * ROWS] = jnp.where(
                kept, flipped, 0.0
            ).astype(BF16)
    own[2].wait()
    arrived(reads, N_DP - 1, recv_sem.at[2])

    for i in range(N_DP):
        block = reads[i].astype(F32)
        for k in range(N_DP):
            kept = keys_col[i] == key_before[k : k + 1, :]
            reads_m[i, :, k * STATE : (k + 1) * STATE] = jnp.where(kept, block, 0.0).astype(BF16)

    ordered = iota((ROWS, ROWS), 0) >= iota((ROWS, ROWS), 1)

    def score_rows(i, carry):
        key_q = keys_col[i][:, 0:1]
        block = reads[i]

        def score(j, carry):
            raw = dot(block, writes[j], ((1,), (1,)))
            kept = (key_q == keys_row[pl.ds(j, 1), :]) & (ordered | (j < i))
            scores[i, :, pl.ds(pl.multiple_of(j * ROWS, ROWS), ROWS)] = jnp.where(
                kept, raw, 0.0
            ).astype(BF16)
            return carry

        return lax.fori_loop(0, i + 1, score, carry)

    lax.fori_loop(0, N_DP, score_rows, 0)

    def summarize(c):
        pltpu.make_async_copy(xs.at[0, 0], xs.at[0, 0], local_sem.at[4 + c]).wait()
        arrived(xs.at[c], N_DP - 1, x_recv.at[c])

        def scale(i, carry):
            factor = dot(factors[i], spread[1, c])
            scaled[c, pl.ds(pl.multiple_of(i * ROWS, ROWS), ROWS), :] = (
                xs[c, i].astype(F32) * factor
            ).astype(BF16)
            return carry

        lax.fori_loop(0, N_DP, scale, 0)

        def collect(k, carry):
            pair = lax.rem(k + col // 4, N_DP // 2)
            part = dot(writes_t[pair], scaled[c])
            for side in range(4):
                peer = 4 * pair + side
                half = aux[
                    2 * pair + side // 2, 1:2, pl.ds(pl.multiple_of(c * WIDTH, WIDTH), WIDTH)
                ]
                sums[c, peer] = (part[64 * side : 64 * side + 64] * half).astype(BF16)

                @pl.when(peer != col)
                def _():
                    remote(
                        sums.at[c, peer], sums_in.at[c, col], s_send.at[c], s_recv.at[c], "ctx", peer
                    ).start()

            return carry

        lax.fori_loop(0, N_DP // 2, collect, 0)
        sums_in[c, col] = sums[c, col]

    def carry_on(c):
        @pl.when(c == 0)
        def _():
            arrived(aux_in, N_CTX - 1, recv_sem.at[3])

        arrived(sums_in.at[c], N_CTX - 1, s_recv.at[c])
        window = pl.ds(pl.multiple_of(c * WIDTH, WIDTH), WIDTH)

        def advance(j, held):
            states[c, j] = (held * aux_in[j, 1:2, window]).astype(BF16)
            return held * aux_in[j, 0:1, window] + sums_in[c, j].astype(F32)

        lax.fori_loop(0, N_CTX, advance, jnp.zeros((64, WIDTH), F32))
        for d in range(1, N_CTX):
            peer = lax.rem(col + d, N_CTX)
            remote(
                states.at[c, peer], states_in.at[c, col], h_send.at[c], h_recv.at[c], "ctx", peer
            ).start()
        states_in[c, col] = states[c, col]

    def hand_back(c, peer):
        remote(
            mixed.at[c, peer], piece(out_ref, me, c), y_send.at[c], y_recv.at[c], "dp", peer
        ).start()

    def look_back(c):
        for i in range(N_DP):
            reach = (i + 1) * ROWS
            inner[c, i] = dot(scores[i, :, 0:reach], scaled[c, 0:reach, :])

    def mix(c):
        arrived(states_in.at[c], N_CTX - 1, h_recv.at[c])
        carried = states_in[c].reshape(N_DP * STATE, WIDTH)
        skip = skips[c, 0:1, :]
        for i in range(N_DP):
            both = inner[c, i] + dot(reads_m[i], carried)
            factor = dot(factors[i], spread[0, c])
            mixed[c, i] = (both * factor + skip * xs[c, i].astype(F32)).astype(BF16)

            @pl.when((me != i) & (c < CHUNKS - 1))
            def _():
                remote(
                    mixed.at[c, i], landed.at[c, me], y_send.at[c], y_recv.at[c], "dp", i
                ).start()

            @pl.when((me != i) & (c == CHUNKS - 1))
            def _():
                remote(
                    mixed.at[c, i], last_ref.at[me], y_send.at[c], y_recv.at[c], "dp", i
                ).start()

        @pl.when(c < CHUNKS - 1)
        def _():
            landed[c, me] = mixed[c, me]

    def step(s, carry):
        @pl.when(s < CHUNKS)
        def _():
            summarize(s)

        @pl.when((s > 0) & (s < CHUNKS + 1))
        def _():
            carry_on(s - 1)

        @pl.when(s > 1)
        def _():
            mix(s - 2)

        @pl.when(s < CHUNKS)
        def _():
            look_back(s)

        return carry

    lax.fori_loop(0, CHUNKS + 2, step, 0)

    last_copy = pltpu.make_async_copy(
        mixed.at[CHUNKS - 1, me], last_ref.at[me], local_sem.at[3]
    )
    last_copy.start()
    gate_copy.wait()
    squares[...] = jnp.zeros((ROWS, 128), F32)
    results = []
    for c in range(CHUNKS - 1):
        arrived(landed.at[c], N_DP - 1, y_recv.at[c])

        def gating(g, carry):
            gate = gates[:, pl.ds(pl.multiple_of(g * 1024 + c * WIDTH, WIDTH), WIDTH)].astype(F32)
            gated = landed[c, g].astype(F32) * silu(gate)
            landed[c, g] = gated.astype(BF16)
            total = jnp.sum(gated * gated, axis=1, keepdims=True)
            squares[...] += jnp.where(iota((ROWS, 128), 1) == g, total, 0.0)
            return carry

        lax.fori_loop(0, GROUPS, gating, 0)
        results.append(pltpu.make_async_copy(landed.at[c], gated_ref.at[c], done_sem.at[c]))
        results[-1].start()
    results.append(pltpu.make_async_copy(squares, squares_ref, done_sem.at[CHUNKS - 1]))
    results[-1].start()
    for copy in results:
        copy.wait()
    last_copy.wait()
    arrived(mixed.at[CHUNKS - 1], N_DP - 1, y_recv.at[CHUNKS - 1])

    arrived(meta, N_DP - 1, send_sem.at[0])
    arrived(writes, N_DP - 1, send_sem.at[1])
    arrived(reads, N_DP - 1, send_sem.at[2])
    arrived(aux_in, N_CTX - 1, send_sem.at[3])
    for c in range(CHUNKS):
        arrived(xs.at[c], N_DP - 1, x_send.at[c])
        arrived(sums_in.at[c], N_CTX - 1, s_send.at[c])
        arrived(states_in.at[c], N_CTX - 1, h_send.at[c])
        arrived(mixed.at[c], N_DP - 1, y_send.at[c])


def finish(
    gated_hbm,
    squares_hbm,
    last_hbm,
    gate_hbm,
    gain_hbm,
    out_ref,
    squares_ref,
    gain_ref,
    gated,
    lasts,
    gates,
    done,
    row_sem,
    load_sem,
    done_sem,
):
    early = WIDTH * (CHUNKS - 1)

    def loads(g):
        start = pl.multiple_of(g * 1024 + early, WIDTH)
        return [
            pltpu.make_async_copy(gate_hbm.at[:, pl.ds(start, WIDTH)], gates.at[g], load_sem.at[0, g]),
            pltpu.make_async_copy(last_hbm.at[g], lasts.at[g], load_sem.at[1, g]),
            pltpu.make_async_copy(gated_hbm.at[:, g], gated.at[g], load_sem.at[2, g]),
        ]

    def result(g):
        place = pl.ds(pl.multiple_of(g * 1024, 1024), 1024)
        return pltpu.make_async_copy(done.at[g], out_ref.at[:, place], done_sem.at[g])

    shared = [
        pltpu.make_async_copy(squares_hbm, squares_ref, row_sem.at[0]),
        pltpu.make_async_copy(gain_hbm, gain_ref, row_sem.at[1]),
    ]
    for copy in loads(0) + shared:
        copy.start()
    for g in range(1, GROUPS):
        for copy in loads(g):
            copy.start()
    for copy in shared:
        copy.wait()

    def group(g, carry):
        for copy in loads(g):
            copy.wait()
        late = lasts[g].astype(F32) * silu(gates[g].astype(F32))
        total = jnp.where(iota((ROWS, 128), 1) == g, squares_ref[...], 0.0)
        for k in range(WIDTH // 128):
            total = total + late[:, k * 128 : (k + 1) * 128] * late[:, k * 128 : (k + 1) * 128]
        inverse = lax.rsqrt(jnp.sum(total, axis=1, keepdims=True) * (1.0 / 1024.0) + EPSILON)
        for c in range(CHUNKS):
            part = gated[g, c].astype(F32) if c < CHUNKS - 1 else late
            gain = gain_ref[:, pl.ds(pl.multiple_of(g * 1024 + c * WIDTH, WIDTH), WIDTH)]
            done[g, :, c * WIDTH : (c + 1) * WIDTH] = (part * inverse * gain).astype(BF16)
        result(g).start()
        return carry

    lax.fori_loop(0, GROUPS, group, 0)
    for g in range(GROUPS):
        result(g).wait()


def shards(
    ssm_input,
    gate_input,
    write_basis,
    read_basis,
    step_size,
    decay_rate,
    skip_weight,
    norm_gain,
    row_owner,
    document_lengths,
):
    hbm = pl.BlockSpec(memory_space=pltpu.HBM)
    anywhere = pl.BlockSpec(memory_space=pl.ANY)
    dma = pltpu.SemaphoreType.DMA
    gated, squares, last = pl.pallas_call(
        kernel,
        out_shape=[
            jax.ShapeDtypeStruct((CHUNKS - 1, GROUPS, ROWS, WIDTH), BF16),
            jax.ShapeDtypeStruct((ROWS, 128), F32),
            jax.ShapeDtypeStruct((GROUPS, ROWS, WIDTH), BF16),
        ],
        in_specs=[hbm] * 9,
        out_specs=[anywhere] * 3,
        scratch_shapes=[
            pltpu.VMEM((ROWS, GROUPS * 1024), BF16),
            pltpu.VMEM((CHUNKS - 1, N_DP, ROWS, WIDTH), BF16),
            pltpu.VMEM((ROWS, 128), F32),
            pltpu.VMEM((1, ROWS), jnp.int32),
            pltpu.VMEM((1, DOCS), jnp.int32),
            pltpu.VMEM((1, 128), F32),
            pltpu.VMEM((1, 128), F32),
            pltpu.VMEM((ROWS, 128), BF16),
            pltpu.VMEM((N_DP, HEADS, ROWS + 128), BF16),
            pltpu.VMEM((CHUNKS, 8, WIDTH), F32),
            pltpu.VMEM((N_DP, HEADS, ROWS + 128), BF16),
            pltpu.VMEM((N_DP, ROWS, STATE), BF16),
            pltpu.VMEM((N_DP, ROWS, STATE), BF16),
            pltpu.VMEM((CHUNKS, N_DP, ROWS, WIDTH), BF16),
            pltpu.VMEM((N_DP, 8, 1024), F32),
            pltpu.VMEM((N_CTX, 8, 1024), F32),
            pltpu.VMEM((CHUNKS, N_CTX, 64, WIDTH), BF16),
            pltpu.VMEM((CHUNKS, N_CTX, 64, WIDTH), BF16),
            pltpu.VMEM((CHUNKS, N_CTX, 64, WIDTH), BF16),
            pltpu.VMEM((CHUNKS, N_CTX, 64, WIDTH), BF16),
            pltpu.VMEM((CHUNKS, N_DP, ROWS, WIDTH), BF16),
            pltpu.VMEM((N_DP, ROWS, N_DP * ROWS), BF16),
            pltpu.VMEM((CHUNKS, N_DP * ROWS, WIDTH), BF16),
            pltpu.VMEM((N_DP // 2, 2 * STATE, N_DP * ROWS), BF16),
            pltpu.VMEM((N_DP, ROWS, N_DP * STATE), BF16),
            pltpu.VMEM((N_DP, ROWS, 128), BF16),
            pltpu.VMEM((N_DP, ROWS), F32),
            pltpu.VMEM((N_DP, ROWS, 128), F32),
            pltpu.VMEM((2, CHUNKS, 128, WIDTH), BF16),
            pltpu.VMEM((CHUNKS, N_DP, ROWS, WIDTH), F32),
            dma((1,)),
            dma((CHUNKS,)),
            dma((4,)),
            dma((4 + CHUNKS,)),
            dma((4,)),
            dma((4,)),
            dma((CHUNKS,)),
            dma((CHUNKS,)),
            dma((CHUNKS,)),
            dma((CHUNKS,)),
            dma((CHUNKS,)),
            dma((CHUNKS,)),
            dma((CHUNKS,)),
            dma((CHUNKS,)),
        ],
        compiler_params=pltpu.CompilerParams(
            collective_id=0, has_side_effects=True, vmem_limit_bytes=60 * 2**20
        ),
        cost_estimate=pl.CostEstimate(
            flops=14 * 10**9, bytes_accessed=16 * 2**20, transcendentals=4 * 10**6
        ),
    )(
        ssm_input,
        write_basis,
        read_basis,
        step_size,
        row_owner.reshape(1, -1),
        document_lengths,
        decay_rate.reshape(1, -1),
        skip_weight.reshape(1, -1),
        gate_input,
    )
    return pl.pallas_call(
        finish,
        out_shape=jax.ShapeDtypeStruct((ROWS, GROUPS * 1024), BF16),
        in_specs=[anywhere] * 5,
        out_specs=anywhere,
        scratch_shapes=[
            pltpu.VMEM((ROWS, 128), F32),
            pltpu.VMEM((1, GROUPS * 1024), F32),
            pltpu.VMEM((GROUPS, CHUNKS - 1, ROWS, WIDTH), BF16),
            pltpu.VMEM((GROUPS, ROWS, WIDTH), BF16),
            pltpu.VMEM((GROUPS, ROWS, WIDTH), BF16),
            pltpu.VMEM((GROUPS, ROWS, 1024), BF16),
            dma((2,)),
            dma((3, GROUPS)),
            dma((GROUPS,)),
        ],
        compiler_params=pltpu.CompilerParams(vmem_limit_bytes=60 * 2**20),
        cost_estimate=pl.CostEstimate(
            flops=20 * 2**20, bytes_accessed=12 * 2**20, transcendentals=2 * 2**20
        ),
    )(gated, squares, last, gate_input, norm_gain.reshape(1, -1))


def solution(mesh):
    placed = (
        P(("dp", "ctx"), None),
        P(("dp", "ctx"), None),
        P(("dp", "ctx"), None),
        P(("dp", "ctx"), None),
        P(("dp", "ctx"), None),
        P(),
        P(),
        P(),
        P(("dp", "ctx"), None),
        P("dp", None),
    )
    return jax.shard_map(
        shards, mesh=mesh, in_specs=placed, out_specs=P(("dp", "ctx"), None), check_vma=False
    )
```
